128 devices in a mesh: elem: 8 (over x, core), rve: 16 (over y, z).
Axes of the slice: x: 4, y: 4, z: 4, core: 2. Of those that a mesh axis runs over, the one named last changes fastest.
Arguments:
- displacement: float32 [3, 256], P(None, ('elem', 'rve')), may hold values from -1.75 to 1.75
- connectivity: int32 [8, 256], P(None, ('elem', 'rve')), may hold values from 0 to 255, as said below
- fluctuation: float32 [2048, 6, 4096], P(('elem', 'rve')), may hold values from -1.75 to 1.75
- phases: int32 [2048, 4096], P(('elem', 'rve')), may hold values from 0 to 2
- damage: float32 [2048, 4096], P(('elem', 'rve')), may hold values from 0 to 0.9
- iteration_counts: int32 [2048], P(('elem', 'rve')), may hold values from 1 to 12
- routing: int32 [2048], P(('elem', 'rve')), may hold values from 0 to 15, as said below
- external_force: float32 [3, 256], P(None, ('elem', 'rve')), may hold values from -6 to 6
Outputs:
- residual_force: float32 [3, 256], P(None, ('elem', 'rve'))
- fluctuation_out: float32 [2048, 6, 4096], P(('elem', 'rve'))
- pool_stress: float32 [2048, 6], P(('elem', 'rve'))
The draws below stay inside these ranges and needn't reach their ends.
Inputs may be any that keep to these rules, and one draw needn't show every extreme that they name: The window is a periodic grid of 4 x 4 x 16 unit elements with renumbered nodes and elements; connectivity[a, e] is the node at corner a = 4 ax + 2 ay + az of element e, offset by ax, ay, az along the three dimensions. `routing`: over the 16 RVEs of one device, a permutation of 0 to 15; value s names pool s // 1 of the same elem index and position s % 1 among that device's RVEs there.
All inputs are finite; a program needn't handle non-finite values.
Results may differ from the reference program's by a relative error of at most 0.0003.
Values sent between devices are 32-bit elements; how exact they have to be, the bound alone decides.
No kernel may reach another device: no remote copies, remote signals or barrier semaphores. Data moves between devices by JAX's collectives and lax.ppermute only.
A program may use at most 64 MiB of HBM per device.

```python
import math
import jax
import jax.numpy as jnp
from jax import lax

NV = 16
MAXIT = 12
GX = 4
GY = 4
VOX = 4096
RVE_DEV = 16
ELEMS = 256
NODES = 256
RVES = 2048
GZ = 16
CAP = 1
N_ELEM = 8
N_RVE = 16


def shared_counts(key):
    home_count = RVES // RVE_DEV
    heat_key, count_key = jax.random.split(key)
    burning = jax.random.randint(heat_key, (home_count,), 0, 4) == 0
    ceiling = jnp.where(burning, MAXIT, MAXIT // 4)
    drawn = jax.random.randint(count_key, (home_count, RVE_DEV), 0, MAXIT)
    counts = 1 + drawn % ceiling[:, None]
    counts = counts.at[0, 0].set(MAXIT)
    return counts.astype(jnp.int32)


def draw_iteration_counts(key, part):
    shared = shared_counts(key)
    return shared.reshape(-1)


def draw_routing(key, part):
    shared = shared_counts(key)
    ordered = jnp.argsort(-shared, axis=1, stable=True)
    ranking = jnp.argsort(ordered, axis=1, stable=True)
    pools = RVE_DEV // CAP
    home_index = jnp.arange(shared.shape[0], dtype=jnp.int32) % pools
    slots = (ranking + home_index[:, None] * CAP) % RVE_DEV
    return slots.reshape(-1).astype(jnp.int32)


def draw_connectivity(key, part):
    key = jax.random.fold_in(key, 13)
    node_key, element_key = jax.random.split(key)
    node_label = jax.random.permutation(node_key, NODES)
    element_order = jax.random.permutation(element_key, ELEMS)
    cell_x = element_order // (GY * GZ)
    cell_y = element_order // GZ % GY
    cell_z = element_order % GZ
    corners = []
    for corner in range(8):
        shift_x = corner >> 2 & 1
        shift_y = corner >> 1 & 1
        shift_z = corner & 1
        lattice = (cell_x + shift_x) % GX * (GY * GZ) + (cell_y + shift_y) % GY * GZ + (cell_z + shift_z) % GZ
        corners.append(node_label[lattice])
    return jnp.stack(corners).astype(jnp.int32)


def set_ends(values, key, low, top_value):
    dims = values.shape
    spot = [jax.random.randint(jax.random.fold_in(key, axis), (), 0, dims[axis]) for axis in range(len(dims))]
    values = values.at[tuple(spot)].set(low)
    longest = dims.index(max(dims))
    spot[longest] = (spot[longest] + 1) % dims[longest]
    return values.at[tuple(spot)].set(top_value)


def level_of(rng, extent, shards, least, largest):
    loudness, own = 1.0, jax.random.fold_in(rng, 6)
    for dim, shards_of in shards:
        heights = jnp.exp(jax.random.uniform(jax.random.fold_in(own, dim), (shards_of,), jnp.float32, least / len(shards), largest / len(shards)))
        loudness = loudness * jnp.repeat(heights, extent[dim] // shards_of).reshape([-1 if axis == dim else 1 for axis in range(len(extent))])
    return loudness


def gaussian(stream_key, dims, width, limit, cuts=(), kind=jnp.bfloat16):
    values = jax.random.normal(stream_key, dims, jnp.float32) * width
    if len(cuts) > 0:
        values = level_of(stream_key, dims, cuts, -0.22, 0.18) * values
    return jnp.clip(values, min=-limit, max=limit).astype(kind)


def setup_inputs(seed: int = 0) -> dict:
    seeds = jax.random.split(jax.random.key(seed), 9)
    displacement = gaussian(seeds[0], (3, NODES), 0.3, 1.75, ((1, 128),), jnp.float32)
    connectivity = draw_connectivity(jax.random.fold_in(seeds[8], 71), 0)
    fluctuation = gaussian(seeds[2], (RVES, 6, VOX), 0.3, 1.75, ((0, 128),), jnp.float32)
    phases = set_ends(jax.random.randint(seeds[3], (RVES, VOX), 0, 3), jax.random.fold_in(seeds[3], 1), 0, 2).astype(jnp.int32)
    damage = jnp.clip(0.9 * jax.random.uniform(seeds[4], (RVES, VOX), jnp.float32) ** level_of(seeds[4], (RVES, VOX), ((0, 128),), -0.2, 0.2), 0.0, 0.9)
    iteration_counts = draw_iteration_counts(jax.random.fold_in(seeds[8], 71), 0)
    routing = draw_routing(jax.random.fold_in(seeds[8], 71), 0)
    external_force = gaussian(seeds[7], (3, NODES), 1.0, 6.0, ((1, 128),), jnp.float32)
    return dict(displacement=displacement, connectivity=connectivity, fluctuation=fluctuation, phases=phases, damage=damage, iteration_counts=iteration_counts, routing=routing, external_force=external_force)


MU_PHASE = (0.1, 0.4, 2.0)
LAM_PHASE = (0.15, 0.6, 1.0)
mu_ref = 1.053
lam_ref = 0.5295
component_pairs = ((0, 0), (1, 1), (2, 2), (1, 2), (0, 2), (0, 1))
component_index = {(0, 0): 0, (1, 1): 1, (2, 2): 2, (1, 2): 3, (2, 1): 3, (0, 2): 4, (2, 0): 4, (0, 1): 5, (1, 0): 5}

def shape_gradients():
    lower_coord = 0.5 - 0.5 / math.sqrt(3.0)
    upper_coord = 0.5 + 0.5 / math.sqrt(3.0)
    gradient_table = []
    for corner in range(8):
        corner_bits = (corner >> 2 & 1, corner >> 1 & 1, corner & 1)
        corner_rows = []
        for point_index in range(8):
            point_bits = (point_index >> 2 & 1, point_index >> 1 & 1, point_index & 1)
            coords = [upper_coord if point_flag else lower_coord for point_flag in point_bits]
            factors = [coords[axis_index] if corner_bits[axis_index] else 1.0 - coords[axis_index] for axis_index in range(3)]
            point_row = []
            for axis_index in range(3):
                entry_value = 1.0 if corner_bits[axis_index] else -1.0
                for other_axis in range(3):
                    if other_axis != axis_index:
                        entry_value = entry_value * factors[other_axis]
                point_row.append(entry_value)
            corner_rows.append(point_row)
        gradient_table.append(corner_rows)
    return gradient_table

def wave_directions():
    line_index = jnp.arange(NV, dtype=jnp.int32)
    wave_line = jnp.where(line_index < (NV + 1) // 2, line_index, line_index - NV).astype(jnp.float32)
    wave_x, wave_y, wave_z = jnp.meshgrid(wave_line, wave_line, wave_line, indexing='ij')
    length = jnp.sqrt(wave_x ** 2 + wave_y ** 2 + wave_z ** 2)
    safe_length = jnp.where(length > 0, length, 1.0)
    return tuple((jnp.where(length > 0, component_wave / safe_length, 0.0) for component_wave in (wave_x, wave_y, wave_z)))

def moduli(phases, damage):
    softening = (1.0 - damage) ** 2 + 0.05
    shear_modulus = sum((jnp.where(phases == phase_level, MU_PHASE[phase_level], 0.0) for phase_level in range(3))) * softening
    lame_modulus = sum((jnp.where(phases == phase_level, LAM_PHASE[phase_level], 0.0) for phase_level in range(3))) * softening
    return (shear_modulus, lame_modulus)

def strain_components(deformation):
    return jnp.stack([0.5 * (deformation[..., first_axis, second_axis] + deformation[..., second_axis, first_axis]) for first_axis, second_axis in component_pairs], axis=-1)

def full_tensor(components):
    rows_list = [jnp.stack([components[..., component_index[row_axis, column_axis]] for column_axis in range(3)], axis=-1) for row_axis in range(3)]
    return jnp.stack(rows_list, axis=-2)

def local_stress(strain, shear_modulus, lame_modulus):
    trace_sum = strain[:, 0] + strain[:, 1] + strain[:, 2]
    pieces = []
    for member in range(6):
        entry_value = 2.0 * shear_modulus * strain[:, member]
        if member < 3:
            entry_value = entry_value + lame_modulus * trace_sum
        pieces.append(entry_value)
    return jnp.stack(pieces, axis=1)

def green_apply(spectra, directions):
    vectors = [sum((spectra[component_index[row_axis, column_axis]] * directions[column_axis] for column_axis in range(3))) for row_axis in range(3)]
    normal = sum((directions[row_axis] * vectors[row_axis] for row_axis in range(3)))
    volume_term = (lam_ref + mu_ref) / (mu_ref * (lam_ref + 2.0 * mu_ref))
    result = []
    for first_axis, second_axis in component_pairs:
        shear_part = (directions[second_axis] * vectors[first_axis] + directions[first_axis] * vectors[second_axis]) / (2.0 * mu_ref)
        result.append(shear_part - volume_term * directions[first_axis] * directions[second_axis] * normal)
    return result

def solve_block(initial, shear_modulus, lame_modulus, macro_strain, counts, directions):

    def sweep(step_index, strain):
        stress_field = local_stress(strain, shear_modulus, lame_modulus)
        spectra = jnp.fft.fftn(stress_field, axes=(2, 3, 4))
        applied = green_apply([spectra[:, member] for member in range(6)], directions)
        update = jnp.real(jnp.fft.ifftn(jnp.stack(applied, axis=1), axes=(2, 3, 4)))
        correction = macro_strain - lax.optimization_barrier(jnp.mean(strain, axis=(2, 3, 4)))
        renewed = strain - update + correction[:, :, None, None, None]
        active = (step_index < counts)[:, None, None, None, None]
        return jnp.where(active, renewed, strain)
    final_strain = lax.fori_loop(0, MAXIT, sweep, initial)
    stress_mean = lax.optimization_barrier(jnp.mean(local_stress(final_strain, shear_modulus, lame_modulus), axis=(2, 3, 4)))
    return (final_strain, stress_mean)

def reference(displacement, connectivity, fluctuation, phases, damage, iteration_counts, routing, external_force):
    gradients = jnp.asarray(shape_gradients(), dtype=jnp.float32)
    directions = tuple((jnp.asarray(direction_table, dtype=jnp.float32) for direction_table in wave_directions()))
    corner_motion = displacement[:, connectivity]
    deformation = jnp.einsum('iae,aqj->eqij', corner_motion, gradients, precision=lax.Precision.HIGHEST)
    macro_strain = strain_components(deformation).reshape(RVES, 6)
    shear_modulus, lame_modulus = moduli(phases, damage)
    groups = RVES // 8
    initial = (fluctuation + macro_strain[:, :, None]).reshape(groups, 8, 6, NV, NV, NV)

    def solve_group(group_data):
        group_start, group_shear, group_lame, group_macro, group_counts = group_data
        return solve_block(group_start, group_shear, group_lame, group_macro, group_counts, directions)
    finals, stresses = lax.map(solve_group, (initial, shear_modulus.reshape(groups, 8, NV, NV, NV), lame_modulus.reshape(groups, 8, NV, NV, NV), macro_strain.reshape(groups, 8, 6), iteration_counts.reshape(groups, 8)))
    final_strain = finals.reshape(RVES, 6, VOX)
    rve_stress = stresses.reshape(RVES, 6)
    fluctuation_out = final_strain - macro_strain[:, :, None]
    stress_tensor = full_tensor(rve_stress).reshape(ELEMS, 8, 3, 3)
    corner_force = 0.125 * jnp.einsum('eqij,aqj->iae', stress_tensor, gradients, precision=lax.Precision.HIGHEST)
    nodal_force = jnp.zeros((3, NODES), jnp.float32).at[:, connectivity.reshape(-1)].add(corner_force.reshape(3, -1))
    residual_force = nodal_force - external_force
    home_count = RVES // RVE_DEV
    slot_range = jnp.arange(RVE_DEV, dtype=jnp.int32)
    slot_match = (routing.reshape(home_count, RVE_DEV)[:, :, None] == slot_range[None, None, :]).astype(jnp.int32)
    inverse = lax.optimization_barrier(jnp.sum(slot_match * slot_range[None, :, None], axis=1)).astype(jnp.int32)
    sent_rows = jnp.take_along_axis(rve_stress.reshape(home_count, RVE_DEV, 6), inverse[:, :, None], axis=1)
    pool_stress = sent_rows.reshape(N_ELEM, N_RVE, N_RVE, CAP, 6).transpose(0, 2, 1, 3, 4).reshape(RVES, 6)
    return (residual_force, fluctuation_out, pool_stress)
```

```python
import math

import jax
import jax.numpy as jnp
import ml_dtypes
import numpy as np
from jax import lax
from jax.experimental import pallas as pl
from jax.experimental.pallas import tpu as pltpu
from jax.sharding import PartitionSpec as P

NV = 16
PLANE = NV * NV
VOX = NV**3
LANES = 128
SLOTS = 8
RVES = 16
ROWS = NV * SLOTS
MU_PHASE = (0.1, 0.4, 2.0)
LAM_PHASE = (0.15, 0.6, 1.0)
mu_ref = 1.053
lam_ref = 0.5295
component_pairs = ((0, 0), (1, 1), (2, 2), (1, 2), (0, 2), (0, 1))
component_index = {tuple(sorted(pair)): c for c, pair in enumerate(component_pairs)}
SQRT2 = math.sqrt(2.0)
MANDEL = (1.0, 1.0, 1.0, SQRT2, SQRT2, SQRT2)
SWAP = (0, 2, 1, 3, 5, 4)
NORMAL_SCALE = (lam_ref + mu_ref) / (lam_ref + 2.0 * mu_ref)
GREEN_SCALE = -2.0 / (mu_ref * VOX)
AXIS_GREEN = {0: 1.0 / (lam_ref + 2.0 * mu_ref), 4: 0.5 / mu_ref, 5: 0.5 / mu_ref}
HIGHEST = lax.Precision.HIGHEST


def shape_gradients():
    lower = 0.5 - 0.5 / math.sqrt(3.0)
    upper = 0.5 + 0.5 / math.sqrt(3.0)
    table = np.zeros((8, 8, 3))
    for corner in range(8):
        bits = (corner >> 2 & 1, corner >> 1 & 1, corner & 1)
        for point in range(8):
            coords = [upper if point >> shift & 1 else lower for shift in (2, 1, 0)]
            factors = [c if b else 1.0 - c for c, b in zip(coords, bits)]
            for axis in range(3):
                entry = 1.0 if bits[axis] else -1.0
                for other in range(3):
                    if other != axis:
                        entry *= factors[other]
                table[corner, point, axis] = entry
    return table


def element_tables():
    gradient = shape_gradients()
    strain = np.zeros((6, RVES, 3, 16))
    force = np.zeros((3, 16, 6, RVES))
    for r in range(RVES):
        e, q = divmod(r, 8)
        for a in range(8):
            j = 2 * a + e
            for c, (k, h) in enumerate(component_pairs):
                strain[c, r, k, j] += 0.5 * gradient[a, q, h]
                strain[c, r, h, j] += 0.5 * gradient[a, q, k]
            for i in range(3):
                for h in range(3):
                    force[i, j, component_index[tuple(sorted((i, h)))], r] += (
                        0.125 * gradient[a, q, h]
                    )
    return strain.reshape(96, 48), force.reshape(48, 96)


def wave(m):
    return m if m < NV // 2 else m - NV


def lane_waves():
    chosen, seen = [], set()
    for ky in range(NV):
        for kz in range(NV):
            partner = (-ky % NV, -kz % NV)
            if (ky, kz) == partner or (ky, kz) in seen:
                continue
            seen.update(((ky, kz), partner))
            chosen.append((ky, kz))
    return chosen


def plane_tables():
    y, z = np.divmod(np.arange(PLANE), NV)
    forward = np.zeros((PLANE, 2 * LANES))
    for lane, (ky, kz) in enumerate(lane_waves()):
        angle = 2.0 * np.pi / NV * ((ky * y + kz * z) % NV)
        forward[:, lane] = np.cos(angle)
        forward[:, LANES + lane] = -np.sin(angle)
    forward[:, 126] = 1.0 - 2.0 * (y % 2)
    forward[:, LANES + 126] = 1.0 - 2.0 * (z % 2)
    forward[:, 127] = 1.0 - 2.0 * ((y + z) % 2)
    forward[:, LANES + 127] = 1.0
    inverse = forward.T.copy()
    inverse[[126, 127, LANES + 126, LANES + 127]] *= 0.5
    return forward, inverse


def split_table(table):
    high = table.astype(ml_dtypes.bfloat16)
    low = (table - high.astype(np.float64)).astype(ml_dtypes.bfloat16)
    return np.concatenate([high, high, low], axis=0)


def green_tables():
    waves = lane_waves() + [(8, 0), (8, 8)]
    out = np.zeros((NV, 12, LANES))
    for kx in range(NV):
        for lane, (ky, kz) in enumerate(waves):
            index = (kx, ky, kz)
            m = np.array([wave(v) for v in index], float)
            back = np.array([wave(-v % NV) for v in index], float)
            length = np.linalg.norm(m)
            if length == 0:
                continue
            n, b = m / length, back / length
            square = n * n
            pair = lambda k, h: 0.5 * (n[k] * n[h] + b[k] * b[h])
            p = [pair(1, 2), pair(0, 2), pair(0, 1)]
            out[kx, 0:3, lane] = square
            out[kx, 3:6, lane] = [v / SQRT2 for v in p]
            for o in range(3):
                k, h = [axis for axis in range(3) if axis != o]
                out[kx, 6 + o, lane] = (
                    0.5 * (square[k] + square[h])
                    - 2.0 * NORMAL_SCALE * square[k] * square[h]
                )
                out[kx, 9 + o, lane] = p[o] * (0.5 - 2.0 * NORMAL_SCALE * square[o])
    return out * GREEN_SCALE


def twiddle(re, im, power, sign):
    power %= 16
    if power == 0:
        return re, im
    if power == 4:
        return (im, -re) if sign < 0 else (-im, re)
    angle = 2.0 * math.pi * power / 16.0
    c, s = math.cos(angle), sign * math.sin(angle)
    if power % 4 == 2:
        root = math.sqrt(0.5)
        cs, ss = math.copysign(1.0, c), math.copysign(1.0, s)
        a = re if cs > 0 else -re
        b = im if cs > 0 else -im
        if cs * ss > 0:
            real, imag = (re - im), (re + im)
        else:
            real, imag = (re + im), (im - re)
        return real * (cs * root), imag * (cs * root)
    return re * c - im * s, re * s + im * c


def dft4(v, sign):
    (ar, ai), (br, bi), (cr, ci), (dr, di) = v
    sr, si, tr, ti = ar + cr, ai + ci, ar - cr, ai - ci
    ur, ui, wr, wi = br + dr, bi + di, br - dr, bi - di
    if sign < 0:
        return [
            (sr + ur, si + ui),
            (tr + wi, ti - wr),
            (sr - ur, si - ui),
            (tr - wi, ti + wr),
        ]
    return [
        (sr + ur, si + ui),
        (tr - wi, ti + wr),
        (sr - ur, si - ui),
        (tr + wi, ti - wr),
    ]


def dft16(values, sign):
    middle = [[None] * 4 for _ in range(4)]
    for first in range(4):
        inner = dft4([values[4 * second + first] for second in range(4)], sign)
        for k in range(4):
            middle[k][first] = twiddle(*inner[k], first * k, sign)
    out = [None] * 16
    for k in range(4):
        outer = dft4(middle[k], sign)
        for high in range(4):
            out[k + 4 * high] = outer[high]
    return out


def green(t, tab):
    double = 2.0 * NORMAL_SCALE / GREEN_SCALE
    xyz = [tab[a] * t[a] for a in range(3)]
    d = (xyz[0] + xyz[1]) + xyz[2]
    o = [tab[3 + a] * t[3 + a] for a in range(3)]
    sums = [o[1] + o[2], o[0] + o[2], o[0] + o[1]]
    s = sums[0] + o[0]
    d2 = d * double
    m = 0.5 * d2 + s * double
    out = [(xyz[a] + sums[a]) - tab[a] * m for a in range(3)]
    for a in range(3):
        k, h = [axis for axis in range(3) if axis != a]
        value = tab[3 + a] * ((t[k] + t[h]) - d2) + tab[6 + a] * t[3 + a]
        value = value + (tab[9 + h] * t[3 + k] + tab[9 + k] * t[3 + h])
        out.append(value)
    return out


def split(value):
    high = value.astype(jnp.bfloat16)
    low = (value - high.astype(jnp.float32)).astype(jnp.bfloat16)
    return high, low


def product(high, low, table_ref):
    left = jnp.concatenate([high, low, high], axis=1)
    return jnp.dot(left, table_ref[...], preferred_element_type=jnp.float32)


def exact(left, right):
    return jnp.dot(left, right, precision=HIGHEST, preferred_element_type=jnp.float32)


def from_scalars(scalars, axis, shape):
    place = lax.broadcasted_iota(jnp.int32, shape, axis)
    out = jnp.full(shape, -1, jnp.int32)
    for index, value in enumerate(scalars):
        out = jnp.where(place == index, value, out)
    return out


def pool_kernel(
    counts,
    routing,
    connectivity,
    elem,
    motion,
    fluctuation,
    phases,
    damage,
    forward,
    inverse,
    tables,
    strain_table,
    force_table,
    fluctuation_out,
    sent,
    order,
    sorted_counts,
    state,
    double_shear,
    lame,
    now_shear,
    now_lame,
    macro,
    now_macro,
    rows,
    parts,
    spectrum,
    table_rows,
    means,
):
    f32 = jnp.float32
    values = [counts[r] for r in range(RVES)]
    for r in range(RVES):
        rank = jnp.int32(0)
        for j in range(RVES):
            if j != r:
                ahead = values[j] >= values[r] if j < r else values[j] > values[r]
                rank = rank + ahead.astype(jnp.int32)
        place = jnp.where(rank < SLOTS, rank, RVES + SLOTS - 1 - rank)
        order[place] = r
        sorted_counts[place] = values[r]
    first = [sorted_counts[s] for s in range(SLOTS)]
    total = [sorted_counts[s] + sorted_counts[SLOTS + s] for s in range(SLOTS)]
    limit = total[0]
    for s in range(1, SLOTS):
        limit = jnp.maximum(limit, total[s])

    nodes = [connectivity[a, e] for a in range(8) for e in range(2)]
    node_rows = from_scalars(nodes, 0, (16, LANES))
    holder = (lax.broadcasted_iota(jnp.int32, (16, LANES), 1) == (node_rows >> 1)).astype(f32)
    corner = exact(holder, motion[...].reshape(LANES, LANES))
    odd = (node_rows & 1) == 1
    moved = [
        jnp.where(
            odd,
            jnp.broadcast_to(corner[:, 3 + i : 4 + i], (16, LANES)),
            jnp.broadcast_to(corner[:, i : i + 1], (16, LANES)),
        )
        for i in range(3)
    ]
    rows[0:96, :] = exact(strain_table[...], jnp.concatenate(moved, axis=0))
    for half in range(2):
        for s in range(SLOTS):
            r = order[half * SLOTS + s]
            for c in range(6):
                macro[half, c, s : s + 1, :] = rows[pl.ds(c * RVES + r, 1), :]

    picked = jnp.concatenate(
        [
            (lax.broadcasted_iota(jnp.int32, (1, RVES), 1) == order[k]).astype(f32)
            for k in range(RVES)
        ],
        axis=0,
    )

    def load(x, carry):
        for side in range(2):
            lanes = pl.ds(pl.multiple_of(x * PLANE + side * LANES, LANES), LANES)
            place = pl.ds(pl.multiple_of(x * SLOTS, SLOTS), SLOTS)
            cut = slice(side * LANES, (side + 1) * LANES)
            phase = exact(picked, phases[:, lanes].astype(f32))
            soft = 1.0 - exact(picked, damage[:, lanes])
            soft = soft * soft + 0.05
            shear = jnp.where(
                phase < 0.5,
                2.0 * MU_PHASE[0],
                jnp.where(phase < 1.5, 2.0 * MU_PHASE[1], 2.0 * MU_PHASE[2]),
            )
            second = jnp.where(
                phase < 0.5,
                LAM_PHASE[0],
                jnp.where(phase < 1.5, LAM_PHASE[1], LAM_PHASE[2]),
            )
            shear, second = shear * soft, second * soft
            for half in range(2):
                double_shear[half, place, cut] = shear[half * SLOTS : (half + 1) * SLOTS]
                lame[half, place, cut] = second[half * SLOTS : (half + 1) * SLOTS]
                block = jnp.stack(
                    [fluctuation[order[half * SLOTS + s], :, lanes] for s in range(SLOTS)], axis=0
                )
                block = jnp.swapaxes(block, 0, 1)
                for c in range(6):
                    state[half, c, place, cut] = (block[c] + macro[half, c]) * MANDEL[c]
        return carry

    lax.fori_loop(0, NV, load, 0)
    now_shear[...] = double_shear[0]
    now_lame[...] = lame[0]
    now_macro[...] = macro[0]
    for kx in range(NV):
        for k in range(12):
            table_rows[kx, k] = jnp.broadcast_to(
                tables[kx * 12 + k : kx * 12 + k + 1, :], (SLOTS, LANES)
            )

    lane = lax.broadcasted_iota(jnp.int32, (SLOTS, LANES), 1)
    first_rows = from_scalars(first, 0, (SLOTS, LANES))
    total_rows = from_scalars(total, 0, (SLOTS, LANES))

    def sweep(step, carry):
        switching = first[0] == step
        ending = total[0] == step
        for s in range(1, SLOTS):
            switching |= first[s] == step
            ending |= total[s] == step

        @pl.when(switching)
        def _():
            mask = first_rows == step
            both = jnp.concatenate([mask, mask], axis=1)

            def exchange(x, inner):
                place = pl.ds(pl.multiple_of(x * SLOTS, SLOTS), SLOTS)
                for c in range(6):
                    old, new = state[0, c, place, :], state[1, c, place, :]
                    state[0, c, place, :] = jnp.where(both, new, old)
                    state[1, c, place, :] = jnp.where(both, old, new)
                now_shear[place, :] = jnp.where(both, double_shear[1, place, :], now_shear[place, :])
                now_lame[place, :] = jnp.where(both, lame[1, place, :], now_lame[place, :])
                return inner

            lax.fori_loop(0, NV, exchange, 0)
            for c in range(6):
                now_macro[c] = jnp.where(mask, macro[1, c], now_macro[c])

        @pl.when(ending)
        def _():
            mask = total_rows == step
            both = jnp.concatenate([mask, mask], axis=1)

            def freeze(x, inner):
                place = pl.ds(pl.multiple_of(x * SLOTS, SLOTS), SLOTS)
                now_shear[place, :] = jnp.where(both, 0.0, now_shear[place, :])
                now_lame[place, :] = jnp.where(both, 0.0, now_lame[place, :])
                return inner

            lax.fori_loop(0, NV, freeze, 0)

        gathered = [None] * 6
        for pair in range(NV // 2):
            place = slice(pair * 16, pair * 16 + 16)
            strain = [state[0, c, place, :] for c in range(6)]
            shear = now_shear[place, :]
            pressure = now_lame[place, :] * ((strain[0] + strain[1]) + strain[2])
            for c in range(6):
                stress = shear * strain[c]
                if c < 3:
                    stress = stress + pressure
                high, low = split(stress)
                parts[c, 0, place, :] = high
                parts[c, 1, place, :] = low
                own = strain[c][:SLOTS] + strain[c][SLOTS:]
                gathered[c] = own if gathered[c] is None else gathered[c] + own
        active = (step < total_rows).astype(f32)
        correction = []
        for c in range(6):
            mean = jnp.sum(gathered[c], axis=1, keepdims=True) * (1.0 / VOX)
            correction.append((now_macro[c] * MANDEL[c] - mean) * active)

        plane = [product(parts[c, 0], parts[c, 1], forward) for c in range(6)]
        for c in range(6):
            line = []
            for x in range(NV):
                place = slice(x * SLOTS, x * SLOTS + SLOTS)
                re, im = plane[c][place, :LANES], plane[c][place, LANES:]
                if SWAP[c] != c:
                    im = jnp.where(lane == 126, plane[SWAP[c]][place, LANES:], im)
                line.append((re, im))
            for kx, (re, im) in enumerate(dft16(line, -1)):
                spectrum[c, kx, 0] = re
                spectrum[c, kx, 1] = im

        axis_values = []
        for c in range(6):
            if c in AXIS_GREEN:
                scale = -2.0 * AXIS_GREEN[c] / PLANE
                offset = 2.0 * correction[c] - (scale / NV) * spectrum[c, 0, 1]
                axis_values.append(
                    [
                        scale * plane[c][x * SLOTS : x * SLOTS + SLOTS, LANES:] + offset
                        for x in range(NV)
                    ]
                )
            else:
                axis_values.append([2.0 * correction[c]] * NV)

        for kx in range(NV):
            tab = [table_rows[kx, k] for k in range(12)]
            for side in range(2):
                out = green([spectrum[c, kx, side] for c in range(6)], tab)
                for c in range(6):
                    spectrum[c, kx, side] = out[c]

        lines = [
            dft16([(spectrum[c, kx, 0], spectrum[c, kx, 1]) for kx in range(NV)], 1)
            for c in range(6)
        ]
        for c in range(6):
            for pair in range(NV // 2):
                re, im = [], []
                for x in (2 * pair, 2 * pair + 1):
                    own = lines[c][x][1]
                    if SWAP[c] != c:
                        own = jnp.where(lane == 126, lines[SWAP[c]][x][1], own)
                    own = jnp.where(lane == 127, axis_values[c][x], own)
                    re.append(lines[c][x][0])
                    im.append(own)
                value = jnp.concatenate(
                    [jnp.concatenate(re, axis=0), jnp.concatenate(im, axis=0)], axis=1
                )
                high, low = split(value)
                parts[c, 0, pair * 16 : pair * 16 + 16, :] = high
                parts[c, 1, pair * 16 : pair * 16 + 16, :] = low
            state[0, c] = state[0, c] + product(parts[c, 0], parts[c, 1], inverse)
        return carry

    lax.fori_loop(0, limit, sweep, 0)

    for half in range(2):
        held = 1 - half

        def gather(x, sums):
            place = pl.ds(pl.multiple_of(x * SLOTS, SLOTS), SLOTS)
            strain = [state[held, c, place, :] for c in range(6)]
            shear = double_shear[half, place, :]
            pressure = lame[half, place, :] * ((strain[0] + strain[1]) + strain[2])
            out = []
            for c in range(6):
                stress = shear * strain[c]
                if c < 3:
                    stress = stress + pressure
                out.append(sums[c] + stress)
            for side in range(2):
                cut = slice(side * LANES, (side + 1) * LANES)
                lanes = pl.ds(pl.multiple_of(x * PLANE + side * LANES, LANES), LANES)
                block = jnp.stack(
                    [
                        strain[c][:, cut] * (1.0 / MANDEL[c]) - macro[half, c]
                        for c in range(6)
                    ],
                    axis=0,
                )
                block = jnp.swapaxes(block, 0, 1)
                for s in range(SLOTS):
                    fluctuation_out[order[half * SLOTS + s], :, lanes] = block[s]
            return tuple(out)

        sums = lax.fori_loop(
            0, NV, gather, tuple(jnp.zeros((SLOTS, PLANE), f32) for _ in range(6))
        )
        for c in range(6):
            mean = jnp.sum(sums[c], axis=1, keepdims=True) * (1.0 / (VOX * MANDEL[c]))
            means[c] = jnp.broadcast_to(mean, (SLOTS, LANES))
        for s in range(SLOTS):
            r = order[half * SLOTS + s]
            for c in range(6):
                rows[pl.ds(c * RVES + r, 1), :] = means[c, s : s + 1, :]

    force = exact(force_table[...], rows[0:96, :])
    column = lax.broadcasted_iota(jnp.int32, (16, LANES), 1)
    right = []
    for low in range(2):
        block = jnp.zeros((16, LANES), f32)
        for i in range(3):
            block = jnp.where(column == 3 * low + i, force[16 * i : 16 * i + 16], block)
        right.append(block)
    block = jnp.zeros((16, LANES), f32)
    for c in range(6):
        block = jnp.where(column == 6 + c, rows[c * RVES : (c + 1) * RVES, :], block)
    right.append(block)
    right.append(jnp.zeros((80, LANES), f32))
    target = [jnp.where((n & 1) == 0, n >> 1, -1) for n in nodes]
    target += [jnp.where((n & 1) == 1, n >> 1, -1) for n in nodes]
    target += [elem[0] * RVES + routing[r] for r in range(RVES)]
    wanted = from_scalars(target, 1, (LANES, LANES))
    taken = (lax.broadcasted_iota(jnp.int32, (LANES, LANES), 0) == wanted).astype(f32)
    sent[...] = exact(taken, jnp.concatenate(right, axis=0)).reshape(LANES, 1, LANES)


def solve(counts, routing, connectivity, elem, motion, fluctuation, phases, damage):
    forward, inverse = (split_table(table) for table in plane_tables())
    strain_table, force_table = element_tables()
    tables = green_tables().reshape(NV * 12, LANES)
    smem = pl.BlockSpec(memory_space=pltpu.SMEM)
    vmem = pl.BlockSpec(memory_space=pltpu.VMEM)
    f32 = jnp.float32
    scratch = [
        pltpu.SMEM((RVES,), jnp.int32),
        pltpu.SMEM((RVES,), jnp.int32),
        pltpu.VMEM((2, 6, ROWS, PLANE), f32),
        pltpu.VMEM((2, ROWS, PLANE), f32),
        pltpu.VMEM((2, ROWS, PLANE), f32),
        pltpu.VMEM((ROWS, PLANE), f32),
        pltpu.VMEM((ROWS, PLANE), f32),
        pltpu.VMEM((2, 6, SLOTS, LANES), f32),
        pltpu.VMEM((6, SLOTS, LANES), f32),
        pltpu.VMEM((96, LANES), f32),
        pltpu.VMEM((6, 2, ROWS, PLANE), jnp.bfloat16),
        pltpu.VMEM((6, NV, 2, SLOTS, LANES), f32),
        pltpu.VMEM((NV, 12, SLOTS, LANES), f32),
        pltpu.VMEM((6, SLOTS, LANES), f32),
    ]
    return pl.pallas_call(
        pool_kernel,
        out_shape=(
            jax.ShapeDtypeStruct((RVES, 6, VOX), f32),
            jax.ShapeDtypeStruct((LANES, 1, LANES), f32),
        ),
        in_specs=[smem] * 4 + [vmem] * 9,
        out_specs=(vmem, vmem),
        scratch_shapes=scratch,
        compiler_params=pltpu.CompilerParams(vmem_limit_bytes=48 * 1024 * 1024),
        name="solve_rves",
    )(
        counts,
        routing,
        connectivity,
        elem,
        motion,
        fluctuation,
        phases,
        damage,
        jnp.asarray(forward),
        jnp.asarray(inverse),
        jnp.asarray(tables, f32),
        jnp.asarray(strain_table, f32),
        jnp.asarray(force_table, f32),
    )


def exchange(rows):
    return lax.all_to_all(rows, ("elem", "rve"), split_axis=0, concat_axis=0, tiled=True)


def shards(
    displacement,
    connectivity,
    fluctuation,
    phases,
    damage,
    iteration_counts,
    routing,
    external_force,
):
    devices = LANES
    own = jnp.pad(displacement.T.reshape(1, 1, 6), ((0, 0), (0, 0), (0, LANES - 6)))
    motion = exchange(jnp.broadcast_to(own, (devices, 1, LANES)))
    elem = lax.axis_index("elem")
    fluctuation_out, sent = solve(
        iteration_counts,
        routing,
        connectivity,
        elem.astype(jnp.int32).reshape(1),
        motion,
        fluctuation,
        phases,
        damage,
    )
    received = exchange(sent)[:, 0, :]
    residual_force = jnp.sum(received[:, :6], axis=0).reshape(2, 3).T - external_force
    pool_stress = lax.dynamic_slice(received, (elem * RVES, 6), (RVES, 6))
    return (residual_force, fluctuation_out, pool_stress)


def solution(mesh):
    both = ("elem", "rve")
    return jax.shard_map(
        shards,
        mesh=mesh,
        in_specs=(
            P(None, both),
            P(None, both),
            P(both, None, None),
            P(both, None),
            P(both, None),
            P(both),
            P(both),
            P(None, both),
        ),
        out_specs=(P(None, both), P(both, None, None), P(both, None)),
        check_vma=False,
    )
```

```python
import math

import jax
import jax.numpy as jnp
import ml_dtypes
import numpy as np
from jax import lax
from jax.experimental import pallas as pl
from jax.experimental.pallas import tpu as pltpu
from jax.sharding import PartitionSpec as P

NV = 16
PLANE = NV * NV
VOX = NV**3
LANES = 128
SLOTS = 8
RVES = 16
ROWS = NV * SLOTS
MU_PHASE = (0.1, 0.4, 2.0)
LAM_PHASE = (0.15, 0.6, 1.0)
mu_ref = 1.053
lam_ref = 0.5295
component_pairs = ((0, 0), (1, 1), (2, 2), (1, 2), (0, 2), (0, 1))
component_index = {tuple(sorted(pair)): c for c, pair in enumerate(component_pairs)}
SQRT2 = math.sqrt(2.0)
MANDEL = (1.0, 1.0, 1.0, SQRT2, SQRT2, SQRT2)
SWAP = (0, 2, 1, 3, 5, 4)
NORMAL_SCALE = (lam_ref + mu_ref) / (lam_ref + 2.0 * mu_ref)
GREEN_SCALE = -2.0 / (mu_ref * VOX)
AXIS_GREEN = {0: 1.0 / (lam_ref + 2.0 * mu_ref), 4: 0.5 / mu_ref, 5: 0.5 / mu_ref}
HIGHEST = lax.Precision.HIGHEST


def shape_gradients():
    lower = 0.5 - 0.5 / math.sqrt(3.0)
    upper = 0.5 + 0.5 / math.sqrt(3.0)
    table = np.zeros((8, 8, 3))
    for corner in range(8):
        bits = (corner >> 2 & 1, corner >> 1 & 1, corner & 1)
        for point in range(8):
            coords = [upper if point >> shift & 1 else lower for shift in (2, 1, 0)]
            factors = [c if b else 1.0 - c for c, b in zip(coords, bits)]
            for axis in range(3):
                entry = 1.0 if bits[axis] else -1.0
                for other in range(3):
                    if other != axis:
                        entry *= factors[other]
                table[corner, point, axis] = entry
    return table


def element_tables():
    gradient = shape_gradients()
    strain = np.zeros((6, RVES, 3, 16))
    force = np.zeros((3, 16, 6, RVES))
    for r in range(RVES):
        e, q = divmod(r, 8)
        for a in range(8):
            j = 2 * a + e
            for c, (k, h) in enumerate(component_pairs):
                strain[c, r, k, j] += 0.5 * gradient[a, q, h]
                strain[c, r, h, j] += 0.5 * gradient[a, q, k]
            for i in range(3):
                for h in range(3):
                    force[i, j, component_index[tuple(sorted((i, h)))], r] += (
                        0.125 * gradient[a, q, h]
                    )
    return strain.reshape(96, 48), force.reshape(48, 96)


def wave(m):
    return m if m < NV // 2 else m - NV


def lane_waves():
    chosen, seen = [], set()
    for ky in range(NV):
        for kz in range(NV):
            partner = (-ky % NV, -kz % NV)
            if (ky, kz) == partner or (ky, kz) in seen:
                continue
            seen.update(((ky, kz), partner))
            chosen.append((ky, kz))
    return chosen


def plane_tables():
    y, z = np.divmod(np.arange(PLANE), NV)
    forward = np.zeros((PLANE, 2 * LANES))
    for lane, (ky, kz) in enumerate(lane_waves()):
        angle = 2.0 * np.pi / NV * ((ky * y + kz * z) % NV)
        forward[:, lane] = np.cos(angle)
        forward[:, LANES + lane] = -np.sin(angle)
    forward[:, 126] = 1.0 - 2.0 * (y % 2)
    forward[:, LANES + 126] = 1.0 - 2.0 * (z % 2)
    forward[:, 127] = 1.0 - 2.0 * ((y + z) % 2)
    forward[:, LANES + 127] = 1.0
    inverse = forward.T.copy()
    inverse[[126, 127, LANES + 126, LANES + 127]] *= 0.5
    return forward, inverse


def split_table(table):
    high = table.astype(ml_dtypes.bfloat16)
    low = (table - high.astype(np.float64)).astype(ml_dtypes.bfloat16)
    return np.concatenate([high, high, low], axis=0)


def green_tables():
    waves = lane_waves() + [(8, 0), (8, 8)]
    out = np.zeros((NV, 12, LANES))
    for kx in range(NV):
        for lane, (ky, kz) in enumerate(waves):
            index = (kx, ky, kz)
            m = np.array([wave(v) for v in index], float)
            back = np.array([wave(-v % NV) for v in index], float)
            length = np.linalg.norm(m)
            if length == 0:
                continue
            n, b = m / length, back / length
            square = n * n
            pair = lambda k, h: 0.5 * (n[k] * n[h] + b[k] * b[h])
            p = [pair(1, 2), pair(0, 2), pair(0, 1)]
            out[kx, 0:3, lane] = square
            out[kx, 3:6, lane] = [v / SQRT2 for v in p]
            for o in range(3):
                k, h = [axis for axis in range(3) if axis != o]
                out[kx, 6 + o, lane] = (
                    0.5 * (square[k] + square[h])
                    - 2.0 * NORMAL_SCALE * square[k] * square[h]
                )
                out[kx, 9 + o, lane] = p[o] * (0.5 - 2.0 * NORMAL_SCALE * square[o])
    return out * GREEN_SCALE


def twiddle(re, im, power, sign):
    power %= 16
    if power == 0:
        return re, im
    if power == 4:
        return (im, -re) if sign < 0 else (-im, re)
    angle = 2.0 * math.pi * power / 16.0
    c, s = math.cos(angle), sign * math.sin(angle)
    if power % 4 == 2:
        root = math.sqrt(0.5)
        cs, ss = math.copysign(1.0, c), math.copysign(1.0, s)
        a = re if cs > 0 else -re
        b = im if cs > 0 else -im
        if cs * ss > 0:
            real, imag = (re - im), (re + im)
        else:
            real, imag = (re + im), (im - re)
        return real * (cs * root), imag * (cs * root)
    return re * c - im * s, re * s + im * c


def dft4(v, sign):
    (ar, ai), (br, bi), (cr, ci), (dr, di) = v
    sr, si, tr, ti = ar + cr, ai + ci, ar - cr, ai - ci
    ur, ui, wr, wi = br + dr, bi + di, br - dr, bi - di
    if sign < 0:
        return [
            (sr + ur, si + ui),
            (tr + wi, ti - wr),
            (sr - ur, si - ui),
            (tr - wi, ti + wr),
        ]
    return [
        (sr + ur, si + ui),
        (tr - wi, ti + wr),
        (sr - ur, si - ui),
        (tr + wi, ti - wr),
    ]


def dft16(values, sign):
    middle = [[None] * 4 for _ in range(4)]
    for first in range(4):
        inner = dft4([values[4 * second + first] for second in range(4)], sign)
        for k in range(4):
            middle[k][first] = twiddle(*inner[k], first * k, sign)
    out = [None] * 16
    for k in range(4):
        outer = dft4(middle[k], sign)
        for high in range(4):
            out[k + 4 * high] = outer[high]
    return out


def green(t, tab):
    double = 2.0 * NORMAL_SCALE / GREEN_SCALE
    xyz = [tab[a] * t[a] for a in range(3)]
    d = (xyz[0] + xyz[1]) + xyz[2]
    o = [tab[3 + a] * t[3 + a] for a in range(3)]
    sums = [o[1] + o[2], o[0] + o[2], o[0] + o[1]]
    s = sums[0] + o[0]
    d2 = d * double
    m = 0.5 * d2 + s * double
    out = [(xyz[a] + sums[a]) - tab[a] * m for a in range(3)]
    for a in range(3):
        k, h = [axis for axis in range(3) if axis != a]
        value = tab[3 + a] * ((t[k] + t[h]) - d2) + tab[6 + a] * t[3 + a]
        value = value + (tab[9 + h] * t[3 + k] + tab[9 + k] * t[3 + h])
        out.append(value)
    return out


def split(value):
    high = value.astype(jnp.bfloat16)
    low = (value - high.astype(jnp.float32)).astype(jnp.bfloat16)
    return high, low


def product(high, low, table_ref):
    left = jnp.concatenate([high, low, high], axis=1)
    return jnp.dot(left, table_ref[...], preferred_element_type=jnp.float32)


def exact(left, right):
    return jnp.dot(left, right, precision=HIGHEST, preferred_element_type=jnp.float32)


def from_scalars(scalars, axis, shape):
    place = lax.broadcasted_iota(jnp.int32, shape, axis)
    out = jnp.full(shape, -1, jnp.int32)
    for index, value in enumerate(scalars):
        out = jnp.where(place == index, value, out)
    return out


def column(values):
    return from_scalars(values, 0, (SLOTS, LANES))


def pick(low, high, rows_of):
    place = rows_of & 7
    low = jnp.take_along_axis(low, place, axis=0, mode="promise_in_bounds")
    high = jnp.take_along_axis(high, place, axis=0, mode="promise_in_bounds")
    return jnp.where(rows_of >= SLOTS, high, low)


def pool_kernel(
    counts,
    routing,
    connectivity,
    elem,
    motion,
    fluctuation,
    phases,
    damage,
    forward,
    inverse,
    tables,
    strain_table,
    force_table,
    fluctuation_out,
    sent,
    order,
    sorted_counts,
    state,
    double_shear,
    lame,
    now_shear,
    now_lame,
    macro,
    now_macro,
    rows,
    parts,
    spectrum,
    table_rows,
    means,
    source,
    where_is,
):
    f32 = jnp.float32
    values = [counts[r] for r in range(RVES)]
    for r in range(RVES):
        rank = jnp.int32(0)
        for j in range(RVES):
            if j != r:
                ahead = values[j] >= values[r] if j < r else values[j] > values[r]
                rank = rank + ahead.astype(jnp.int32)
        place = jnp.where(rank < SLOTS, rank, RVES + SLOTS - 1 - rank)
        order[place] = r
        sorted_counts[place] = values[r]
    first = [sorted_counts[s] for s in range(SLOTS)]
    total = [sorted_counts[s] + sorted_counts[SLOTS + s] for s in range(SLOTS)]
    limit = total[0]
    for s in range(1, SLOTS):
        limit = jnp.maximum(limit, total[s])

    nodes = [connectivity[a, e] for a in range(8) for e in range(2)]
    node_rows = from_scalars(nodes, 0, (16, LANES))
    holder = (lax.broadcasted_iota(jnp.int32, (16, LANES), 1) == (node_rows >> 1)).astype(f32)
    corner = exact(holder, motion[...].reshape(LANES, LANES))
    odd = (node_rows & 1) == 1
    moved = [
        jnp.where(
            odd,
            jnp.broadcast_to(corner[:, 3 + i : 4 + i], (16, LANES)),
            jnp.broadcast_to(corner[:, i : i + 1], (16, LANES)),
        )
        for i in range(3)
    ]
    rows[0:96, :] = exact(strain_table[...], jnp.concatenate(moved, axis=0))
    for half in range(2):
        source[half] = column([order[half * SLOTS + s] for s in range(SLOTS)])
        for c in range(6):
            low = rows[c * RVES : c * RVES + SLOTS, :]
            high = rows[c * RVES + SLOTS : (c + 1) * RVES, :]
            macro[half, c] = pick(low, high, source[half])

    def load(x, carry):
        for side in range(2):
            lanes = pl.ds(pl.multiple_of(x * PLANE + side * LANES, LANES), LANES)
            place = pl.ds(pl.multiple_of(x * SLOTS, SLOTS), SLOTS)
            cut = slice(side * LANES, (side + 1) * LANES)
            phase = phases[:, lanes]
            soft = 1.0 - damage[:, lanes]
            soft = soft * soft + 0.05
            shear = soft * jnp.where(
                phase == 0,
                2.0 * MU_PHASE[0],
                jnp.where(phase == 1, 2.0 * MU_PHASE[1], 2.0 * MU_PHASE[2]),
            )
            second = soft * jnp.where(
                phase == 0, LAM_PHASE[0], jnp.where(phase == 1, LAM_PHASE[1], LAM_PHASE[2])
            )
            for half in range(2):
                rows_of = source[half]
                double_shear[half, place, cut] = pick(shear[:SLOTS], shear[SLOTS:], rows_of)
                lame[half, place, cut] = pick(second[:SLOTS], second[SLOTS:], rows_of)
                for c in range(6):
                    block = pick(
                        fluctuation[c, :SLOTS, lanes], fluctuation[c, SLOTS:, lanes], rows_of
                    )
                    state[half, c, place, cut] = (block + macro[half, c]) * MANDEL[c]
        return carry

    lax.fori_loop(0, NV, load, 0)
    now_shear[...] = double_shear[0]
    now_lame[...] = lame[0]
    now_macro[...] = macro[0]
    for kx in range(NV):
        for k in range(12):
            table_rows[kx, k] = jnp.broadcast_to(
                tables[kx * 12 + k : kx * 12 + k + 1, :], (SLOTS, LANES)
            )

    lane = lax.broadcasted_iota(jnp.int32, (SLOTS, LANES), 1)
    first_rows = from_scalars(first, 0, (SLOTS, LANES))
    total_rows = from_scalars(total, 0, (SLOTS, LANES))

    def sweep(step, carry):
        switching = first[0] == step
        ending = total[0] == step
        for s in range(1, SLOTS):
            switching |= first[s] == step
            ending |= total[s] == step

        @pl.when(switching)
        def _():
            mask = first_rows == step
            both = jnp.concatenate([mask, mask], axis=1)

            def exchange(x, inner):
                place = pl.ds(pl.multiple_of(x * SLOTS, SLOTS), SLOTS)
                for c in range(6):
                    old, new = state[0, c, place, :], state[1, c, place, :]
                    state[0, c, place, :] = jnp.where(both, new, old)
                    state[1, c, place, :] = jnp.where(both, old, new)
                now_shear[place, :] = jnp.where(both, double_shear[1, place, :], now_shear[place, :])
                now_lame[place, :] = jnp.where(both, lame[1, place, :], now_lame[place, :])
                return inner

            lax.fori_loop(0, NV, exchange, 0)
            for c in range(6):
                now_macro[c] = jnp.where(mask, macro[1, c], now_macro[c])

        @pl.when(ending)
        def _():
            mask = total_rows == step
            both = jnp.concatenate([mask, mask], axis=1)

            def freeze(x, inner):
                place = pl.ds(pl.multiple_of(x * SLOTS, SLOTS), SLOTS)
                now_shear[place, :] = jnp.where(both, 0.0, now_shear[place, :])
                now_lame[place, :] = jnp.where(both, 0.0, now_lame[place, :])
                return inner

            lax.fori_loop(0, NV, freeze, 0)

        gathered = [None] * 6
        for pair in range(NV // 2):
            place = slice(pair * 16, pair * 16 + 16)
            strain = [state[0, c, place, :] for c in range(6)]
            shear = now_shear[place, :]
            pressure = now_lame[place, :] * ((strain[0] + strain[1]) + strain[2])
            for c in range(6):
                stress = shear * strain[c]
                if c < 3:
                    stress = stress + pressure
                high, low = split(stress)
                parts[c, 0, place, :] = high
                parts[c, 1, place, :] = low
                own = strain[c][:SLOTS] + strain[c][SLOTS:]
                gathered[c] = own if gathered[c] is None else gathered[c] + own
        active = (step < total_rows).astype(f32)
        correction = []
        for c in range(6):
            mean = jnp.sum(gathered[c], axis=1, keepdims=True) * (1.0 / VOX)
            correction.append((now_macro[c] * MANDEL[c] - mean) * active)

        plane = [product(parts[c, 0], parts[c, 1], forward) for c in range(6)]
        for c in range(6):
            line = []
            for x in range(NV):
                place = slice(x * SLOTS, x * SLOTS + SLOTS)
                re, im = plane[c][place, :LANES], plane[c][place, LANES:]
                if SWAP[c] != c:
                    im = jnp.where(lane == 126, plane[SWAP[c]][place, LANES:], im)
                line.append((re, im))
            for kx, (re, im) in enumerate(dft16(line, -1)):
                spectrum[c, kx, 0] = re
                spectrum[c, kx, 1] = im

        axis_values = []
        for c in range(6):
            if c in AXIS_GREEN:
                scale = -2.0 * AXIS_GREEN[c] / PLANE
                offset = 2.0 * correction[c] - (scale / NV) * spectrum[c, 0, 1]
                axis_values.append(
                    [
                        scale * plane[c][x * SLOTS : x * SLOTS + SLOTS, LANES:] + offset
                        for x in range(NV)
                    ]
                )
            else:
                axis_values.append([2.0 * correction[c]] * NV)

        for kx in range(NV):
            tab = [table_rows[kx, k] for k in range(12)]
            for side in range(2):
                out = green([spectrum[c, kx, side] for c in range(6)], tab)
                for c in range(6):
                    spectrum[c, kx, side] = out[c]

        lines = [
            dft16([(spectrum[c, kx, 0], spectrum[c, kx, 1]) for kx in range(NV)], 1)
            for c in range(6)
        ]
        for c in range(6):
            for pair in range(NV // 2):
                re, im = [], []
                for x in (2 * pair, 2 * pair + 1):
                    own = lines[c][x][1]
                    if SWAP[c] != c:
                        own = jnp.where(lane == 126, lines[SWAP[c]][x][1], own)
                    own = jnp.where(lane == 127, axis_values[c][x], own)
                    re.append(lines[c][x][0])
                    im.append(own)
                value = jnp.concatenate(
                    [jnp.concatenate(re, axis=0), jnp.concatenate(im, axis=0)], axis=1
                )
                high, low = split(value)
                parts[c, 0, pair * 16 : pair * 16 + 16, :] = high
                parts[c, 1, pair * 16 : pair * 16 + 16, :] = low
            state[0, c] = state[0, c] + product(parts[c, 0], parts[c, 1], inverse)
        return carry

    lax.fori_loop(0, limit, sweep, 0)

    def gather(x, sums):
        place = pl.ds(pl.multiple_of(x * SLOTS, SLOTS), SLOTS)
        out = []
        for half in range(2):
            strain = [state[1 - half, c, place, :] for c in range(6)]
            shear = double_shear[half, place, :]
            pressure = lame[half, place, :] * ((strain[0] + strain[1]) + strain[2])
            for c in range(6):
                stress = shear * strain[c]
                if c < 3:
                    stress = stress + pressure
                out.append(sums[6 * half + c] + (stress[:, :LANES] + stress[:, LANES:]))
                state[1 - half, c, place, :] = strain[c] * (1.0 / MANDEL[c])
        for side in range(2):
            cut = slice(side * LANES, (side + 1) * LANES)
            lanes = pl.ds(pl.multiple_of(x * PLANE + side * LANES, LANES), LANES)
            for block in range(2):
                rows_of = source[2 + block]
                for c in range(6):
                    ends = [
                        state[1 - half, c, place, cut] - macro[half, c] for half in range(2)
                    ]
                    fluctuation_out[c, block * SLOTS : (block + 1) * SLOTS, lanes] = pick(
                        *ends, rows_of
                    )
        return tuple(out)

    for r in range(RVES):
        where_is[order[r]] = r
    for block in range(2):
        source[2 + block] = column([where_is[block * SLOTS + s] for s in range(SLOTS)])
    sums = lax.fori_loop(
        0, NV, gather, tuple(jnp.zeros((SLOTS, LANES), f32) for _ in range(12))
    )
    for half in range(2):
        for c in range(6):
            mean = jnp.sum(sums[6 * half + c], axis=1, keepdims=True)
            mean = mean * (1.0 / (VOX * MANDEL[c]))
            means[half, c] = jnp.broadcast_to(mean, (SLOTS, LANES))
    for block in range(2):
        for c in range(6):
            base = c * RVES + block * SLOTS
            rows[base : base + SLOTS, :] = pick(means[0, c], means[1, c], source[2 + block])

    force = exact(force_table[...], rows[0:96, :])
    lane_of = lax.broadcasted_iota(jnp.int32, (16, LANES), 1)
    right = []
    for low in range(2):
        block = jnp.zeros((16, LANES), f32)
        for i in range(3):
            block = jnp.where(lane_of == 3 * low + i, force[16 * i : 16 * i + 16], block)
        right.append(block)
    block = jnp.zeros((16, LANES), f32)
    for c in range(6):
        block = jnp.where(lane_of == 6 + c, rows[c * RVES : (c + 1) * RVES, :], block)
    right.append(block)
    right.append(jnp.zeros((80, LANES), f32))
    target = [jnp.where((n & 1) == 0, n >> 1, -1) for n in nodes]
    target += [jnp.where((n & 1) == 1, n >> 1, -1) for n in nodes]
    target += [elem[0] * RVES + routing[r] for r in range(RVES)]
    wanted = from_scalars(target, 1, (LANES, LANES))
    taken = (lax.broadcasted_iota(jnp.int32, (LANES, LANES), 0) == wanted).astype(f32)
    sent[...] = exact(taken, jnp.concatenate(right, axis=0)).reshape(LANES, 1, LANES)


def solve(counts, routing, connectivity, elem, motion, fluctuation, phases, damage):
    forward, inverse = (split_table(table) for table in plane_tables())
    strain_table, force_table = element_tables()
    tables = green_tables().reshape(NV * 12, LANES)
    smem = pl.BlockSpec(memory_space=pltpu.SMEM)
    vmem = pl.BlockSpec(memory_space=pltpu.VMEM)
    f32 = jnp.float32
    scratch = [
        pltpu.SMEM((RVES,), jnp.int32),
        pltpu.SMEM((RVES,), jnp.int32),
        pltpu.VMEM((2, 6, ROWS, PLANE), f32),
        pltpu.VMEM((2, ROWS, PLANE), f32),
        pltpu.VMEM((2, ROWS, PLANE), f32),
        pltpu.VMEM((ROWS, PLANE), f32),
        pltpu.VMEM((ROWS, PLANE), f32),
        pltpu.VMEM((2, 6, SLOTS, LANES), f32),
        pltpu.VMEM((6, SLOTS, LANES), f32),
        pltpu.VMEM((96, LANES), f32),
        pltpu.VMEM((6, 2, ROWS, PLANE), jnp.bfloat16),
        pltpu.VMEM((6, NV, 2, SLOTS, LANES), f32),
        pltpu.VMEM((NV, 12, SLOTS, LANES), f32),
        pltpu.VMEM((2, 6, SLOTS, LANES), f32),
        pltpu.VMEM((4, SLOTS, LANES), jnp.int32),
        pltpu.SMEM((RVES,), jnp.int32),
    ]
    return pl.pallas_call(
        pool_kernel,
        out_shape=(
            jax.ShapeDtypeStruct((6, RVES, VOX), f32),
            jax.ShapeDtypeStruct((LANES, 1, LANES), f32),
        ),
        in_specs=[smem] * 4 + [vmem] * 9,
        out_specs=(vmem, vmem),
        scratch_shapes=scratch,
        compiler_params=pltpu.CompilerParams(vmem_limit_bytes=48 * 1024 * 1024),
        name="solve_rves",
    )(
        counts,
        routing,
        connectivity,
        elem,
        motion,
        fluctuation,
        phases,
        damage,
        jnp.asarray(forward),
        jnp.asarray(inverse),
        jnp.asarray(tables, f32),
        jnp.asarray(strain_table, f32),
        jnp.asarray(force_table, f32),
    )


def exchange(rows):
    return lax.all_to_all(rows, ("elem", "rve"), split_axis=0, concat_axis=0, tiled=True)


def shards(
    displacement,
    connectivity,
    fluctuation,
    phases,
    damage,
    iteration_counts,
    routing,
    external_force,
):
    devices = LANES
    own = jnp.pad(displacement.T.reshape(1, 1, 6), ((0, 0), (0, 0), (0, LANES - 6)))
    motion = exchange(jnp.broadcast_to(own, (devices, 1, LANES)))
    elem = lax.axis_index("elem")
    fluctuation_out, sent = solve(
        iteration_counts,
        routing,
        connectivity,
        elem.astype(jnp.int32).reshape(1),
        motion,
        jnp.transpose(fluctuation, (1, 0, 2)),
        phases,
        damage,
    )
    fluctuation_out = jnp.transpose(fluctuation_out, (1, 0, 2))
    received = exchange(sent)[:, 0, :]
    residual_force = jnp.sum(received[:, :6], axis=0).reshape(2, 3).T - external_force
    pool_stress = lax.dynamic_slice(received, (elem * RVES, 6), (RVES, 6))
    return (residual_force, fluctuation_out, pool_stress)


def solution(mesh):
    both = ("elem", "rve")
    return jax.shard_map(
        shards,
        mesh=mesh,
        in_specs=(
            P(None, both),
            P(None, both),
            P(both, None, None),
            P(both, None),
            P(both, None),
            P(both),
            P(both),
            P(None, both),
        ),
        out_specs=(P(None, both), P(both, None, None), P(both, None)),
        check_vma=False,
    )
```

```python
import math

import jax
import jax.numpy as jnp
import ml_dtypes
import numpy as np
from jax import lax
from jax.experimental import pallas as pl
from jax.experimental.pallas import tpu as pltpu
from jax.sharding import PartitionSpec as P

NV = 16
PLANE = NV * NV
VOX = NV**3
LANES = 128
SLOTS = 8
RVES = 16
ROWS = NV * SLOTS
MU_PHASE = (0.1, 0.4, 2.0)
LAM_PHASE = (0.15, 0.6, 1.0)
mu_ref = 1.053
lam_ref = 0.5295
component_pairs = ((0, 0), (1, 1), (2, 2), (1, 2), (0, 2), (0, 1))
component_index = {tuple(sorted(pair)): c for c, pair in enumerate(component_pairs)}
SQRT2 = math.sqrt(2.0)
MANDEL = (1.0, 1.0, 1.0, SQRT2, SQRT2, SQRT2)
SWAP = (0, 2, 1, 3, 5, 4)
NORMAL_SCALE = (lam_ref + mu_ref) / (lam_ref + 2.0 * mu_ref)
GREEN_SCALE = 2.0 * NORMAL_SCALE
INVERSE_SCALE = -2.0 / (mu_ref * VOX) / GREEN_SCALE
AXIS_SCALE = -2.0 / PLANE / INVERSE_SCALE
OFFSET_SCALE = 2.0 / INVERSE_SCALE
AXIS_GREEN = {0: 1.0 / (lam_ref + 2.0 * mu_ref), 4: 0.5 / mu_ref, 5: 0.5 / mu_ref}
HIGHEST = lax.Precision.HIGHEST


def shape_gradients():
    lower = 0.5 - 0.5 / math.sqrt(3.0)
    upper = 0.5 + 0.5 / math.sqrt(3.0)
    table = np.zeros((8, 8, 3))
    for corner in range(8):
        bits = (corner >> 2 & 1, corner >> 1 & 1, corner & 1)
        for point in range(8):
            coords = [upper if point >> shift & 1 else lower for shift in (2, 1, 0)]
            factors = [c if b else 1.0 - c for c, b in zip(coords, bits)]
            for axis in range(3):
                entry = 1.0 if bits[axis] else -1.0
                for other in range(3):
                    if other != axis:
                        entry *= factors[other]
                table[corner, point, axis] = entry
    return table


def element_tables():
    gradient = shape_gradients()
    strain = np.zeros((6, RVES, 3, 16))
    force = np.zeros((3, 16, 6, RVES))
    for r in range(RVES):
        e, q = divmod(r, 8)
        for a in range(8):
            j = 2 * a + e
            for c, (k, h) in enumerate(component_pairs):
                strain[c, r, k, j] += 0.5 * gradient[a, q, h]
                strain[c, r, h, j] += 0.5 * gradient[a, q, k]
            for i in range(3):
                for h in range(3):
                    force[i, j, component_index[tuple(sorted((i, h)))], r] += (
                        0.125 * gradient[a, q, h]
                    )
    return strain.reshape(96, 48), force.reshape(48, 96)


def wave(m):
    return m if m < NV // 2 else m - NV


def lane_waves():
    chosen, seen = [], set()
    for ky in range(NV):
        for kz in range(NV):
            partner = (-ky % NV, -kz % NV)
            if (ky, kz) == partner or (ky, kz) in seen:
                continue
            seen.update(((ky, kz), partner))
            chosen.append((ky, kz))
    return chosen


def plane_tables():
    y, z = np.divmod(np.arange(PLANE), NV)
    forward = np.zeros((PLANE, 2 * LANES))
    for lane, (ky, kz) in enumerate(lane_waves()):
        angle = 2.0 * np.pi / NV * ((ky * y + kz * z) % NV)
        forward[:, lane] = np.cos(angle)
        forward[:, LANES + lane] = -np.sin(angle)
    forward[:, 126] = 1.0 - 2.0 * (y % 2)
    forward[:, LANES + 126] = 1.0 - 2.0 * (z % 2)
    forward[:, 127] = 1.0 - 2.0 * ((y + z) % 2)
    forward[:, LANES + 127] = 1.0
    inverse = forward.T.copy()
    inverse[[126, 127, LANES + 126, LANES + 127]] *= 0.5
    return forward, inverse * INVERSE_SCALE


def split_table(table):
    high = table.astype(ml_dtypes.bfloat16)
    low = (table - high.astype(np.float64)).astype(ml_dtypes.bfloat16)
    return np.concatenate([high, high, low], axis=0)


def green_tables():
    waves = lane_waves() + [(8, 0), (8, 8)]
    out = np.zeros((NV, 12, LANES))
    for kx in range(NV):
        for lane, (ky, kz) in enumerate(waves):
            index = (kx, ky, kz)
            m = np.array([wave(v) for v in index], float)
            back = np.array([wave(-v % NV) for v in index], float)
            length = np.linalg.norm(m)
            if length == 0:
                continue
            n, b = m / length, back / length
            square = n * n
            pair = lambda k, h: 0.5 * (n[k] * n[h] + b[k] * b[h])
            p = [pair(1, 2), pair(0, 2), pair(0, 1)]
            out[kx, 0:3, lane] = square
            out[kx, 3:6, lane] = [v / SQRT2 for v in p]
            for o in range(3):
                k, h = [axis for axis in range(3) if axis != o]
                out[kx, 6 + o, lane] = (
                    0.5 * (square[k] + square[h])
                    - 2.0 * NORMAL_SCALE * square[k] * square[h]
                )
                out[kx, 9 + o, lane] = p[o] * (0.5 - 2.0 * NORMAL_SCALE * square[o])
    return out * GREEN_SCALE


def twiddle(re, im, power, sign):
    power %= 16
    if power == 0:
        return re, im
    if power == 4:
        return (im, -re) if sign < 0 else (-im, re)
    angle = 2.0 * math.pi * power / 16.0
    c, s = math.cos(angle), sign * math.sin(angle)
    if power % 4 == 2:
        root = math.sqrt(0.5)
        cs, ss = math.copysign(1.0, c), math.copysign(1.0, s)
        a = re if cs > 0 else -re
        b = im if cs > 0 else -im
        if cs * ss > 0:
            real, imag = (re - im), (re + im)
        else:
            real, imag = (re + im), (im - re)
        return real * (cs * root), imag * (cs * root)
    return re * c - im * s, re * s + im * c


def dft4(v, sign):
    (ar, ai), (br, bi), (cr, ci), (dr, di) = v
    sr, si, tr, ti = ar + cr, ai + ci, ar - cr, ai - ci
    ur, ui, wr, wi = br + dr, bi + di, br - dr, bi - di
    if sign < 0:
        return [
            (sr + ur, si + ui),
            (tr + wi, ti - wr),
            (sr - ur, si - ui),
            (tr - wi, ti + wr),
        ]
    return [
        (sr + ur, si + ui),
        (tr - wi, ti + wr),
        (sr - ur, si - ui),
        (tr + wi, ti - wr),
    ]


def dft16_first(values, first, sign):
    inner = dft4(values, sign)
    return [twiddle(*inner[k], first * k, sign) for k in range(4)]


def green(t, tab):
    xyz = [tab[a] * t[a] for a in range(3)]
    d = (xyz[0] + xyz[1]) + xyz[2]
    o = [tab[3 + a] * t[3 + a] for a in range(3)]
    sums = [o[1] + o[2], o[0] + o[2], o[0] + o[1]]
    s = sums[0] + o[0]
    m = 0.5 * d + s
    out = [(xyz[a] + sums[a]) - tab[a] * m for a in range(3)]
    for a in range(3):
        k, h = [axis for axis in range(3) if axis != a]
        value = tab[3 + a] * ((t[k] + t[h]) - d) + tab[6 + a] * t[3 + a]
        value = value + (tab[9 + h] * t[3 + k] + tab[9 + k] * t[3 + h])
        out.append(value)
    return out


def split(value):
    high = value.astype(jnp.bfloat16)
    low = (value - high.astype(jnp.float32)).astype(jnp.bfloat16)
    return high, low


def product(high, low, table_ref):
    left = jnp.concatenate([high, low, high], axis=1)
    return jnp.dot(left, table_ref[...], preferred_element_type=jnp.float32)


def exact(left, right):
    return jnp.dot(left, right, precision=HIGHEST, preferred_element_type=jnp.float32)


def from_scalars(scalars, axis, shape):
    place = lax.broadcasted_iota(jnp.int32, shape, axis)
    out = jnp.full(shape, -1, jnp.int32)
    for index, value in enumerate(scalars):
        out = jnp.where(place == index, value, out)
    return out


def column(values):
    return from_scalars(values, 0, (SLOTS, LANES))


def pick(low, high, rows_of):
    place = rows_of & 7
    low = jnp.take_along_axis(low, place, axis=0, mode="promise_in_bounds")
    high = jnp.take_along_axis(high, place, axis=0, mode="promise_in_bounds")
    return jnp.where(rows_of >= SLOTS, high, low)


def pool_kernel(
    counts,
    routing,
    connectivity,
    elem,
    motion,
    fluctuation_in,
    phases_in,
    damage_in,
    plane_tables_in,
    line_tables_in,
    fluctuation_home,
    sent,
    order,
    sorted_counts,
    state,
    double_shear,
    lame,
    macro,
    rows,
    parts,
    stresses,
    plane,
    back,
    lines,
    back_lines,
    correction,
    offsets,
    table_rows,
    means,
    source,
    where_is,
    fluctuation,
    phases,
    damage,
    both_planes,
    line_tables,
    in_done,
    out_done,
):
    f32 = jnp.float32
    arrivals = [
        pltpu.make_async_copy(start, end, in_done.at[n])
        for n, (start, end) in enumerate(
            [(line_tables_in, line_tables)]
            + [(fluctuation_in.at[c], fluctuation.at[c]) for c in range(6)]
            + [(phases_in, phases), (damage_in, damage), (plane_tables_in, both_planes)]
        )
    ]
    for arrival in arrivals:
        arrival.start()
    forward, inverse = both_planes.at[0], both_planes.at[1]
    fluctuation_out = fluctuation
    values = [counts[r] for r in range(RVES)]
    for r in range(RVES):
        rank = jnp.int32(0)
        for j in range(RVES):
            if j != r:
                ahead = values[j] >= values[r] if j < r else values[j] > values[r]
                rank = rank + ahead.astype(jnp.int32)
        place = jnp.where(rank < SLOTS, rank, RVES + SLOTS - 1 - rank)
        order[place] = r
        sorted_counts[place] = values[r]
    first = [sorted_counts[s] for s in range(SLOTS)]
    total = [sorted_counts[s] + sorted_counts[SLOTS + s] for s in range(SLOTS)]
    limit = total[0]
    for s in range(1, SLOTS):
        limit = jnp.maximum(limit, total[s])

    nodes = [connectivity[a, e] for a in range(8) for e in range(2)]
    node_rows = from_scalars(nodes, 0, (16, LANES))
    holder = (lax.broadcasted_iota(jnp.int32, (16, LANES), 1) == (node_rows >> 1)).astype(f32)
    corner = exact(holder, motion[...].reshape(LANES, LANES))
    odd = (node_rows & 1) == 1
    moved = [
        jnp.where(
            odd,
            jnp.broadcast_to(corner[:, 3 + i : 4 + i], (16, LANES)),
            jnp.broadcast_to(corner[:, i : i + 1], (16, LANES)),
        )
        for i in range(3)
    ]
    arrivals[0].wait()
    moved = jnp.concatenate(moved + [jnp.zeros((LANES - 48, LANES), f32)], axis=0)
    rows[0:96, :] = exact(line_tables[NV * 12 : NV * 12 + 96, :], moved)
    for half in range(2):
        source[half] = column([order[half * SLOTS + s] for s in range(SLOTS)])
        for c in range(6):
            low = rows[c * RVES : c * RVES + SLOTS, :]
            high = rows[c * RVES + SLOTS : (c + 1) * RVES, :]
            macro[half, c] = pick(low, high, source[half])

    def load(x, carry):
        for side in range(2):
            lanes = pl.ds(pl.multiple_of(x * PLANE + side * LANES, LANES), LANES)
            place = pl.ds(pl.multiple_of(((x & 3) * 4 + (x >> 2)) * SLOTS, SLOTS), SLOTS)
            cut = slice(side * LANES, (side + 1) * LANES)
            phase = phases[:, lanes]
            soft = 1.0 - damage[:, lanes]
            soft = soft * soft + 0.05
            shear = soft * jnp.where(
                phase == 0,
                2.0 * MU_PHASE[0],
                jnp.where(phase == 1, 2.0 * MU_PHASE[1], 2.0 * MU_PHASE[2]),
            )
            second = soft * jnp.where(
                phase == 0, LAM_PHASE[0], jnp.where(phase == 1, LAM_PHASE[1], LAM_PHASE[2])
            )
            for half in range(2):
                rows_of = source[half]
                double_shear[half, place, cut] = pick(shear[:SLOTS], shear[SLOTS:], rows_of)
                lame[half, place, cut] = pick(second[:SLOTS], second[SLOTS:], rows_of)
                for c in range(6):
                    block = pick(
                        fluctuation[c, :SLOTS, lanes], fluctuation[c, SLOTS:, lanes], rows_of
                    )
                    state[half, c, place, cut] = (block + macro[half, c]) * MANDEL[c]
        return carry

    for kx in range(NV):
        for k in range(12):
            table_rows[kx, k] = jnp.broadcast_to(
                line_tables[kx * 12 + k : kx * 12 + k + 1, :], (SLOTS, LANES)
            )
    for arrival in arrivals[1:9]:
        arrival.wait()
    lax.fori_loop(0, NV, load, 0)
    arrivals[9].wait()

    lane = lax.broadcasted_iota(jnp.int32, (SLOTS, LANES), 1)
    first_rows = column(first)
    total_rows = column(total)

    scales = [AXIS_SCALE * AXIS_GREEN.get(c, 0.0) for c in range(6)]

    def wave_part(k):
        waves = []
        for c in range(6):
            out = dft4([(lines[c, k, first, 0], lines[c, k, first, 1]) for first in range(4)], -1)
            if k == 0:
                offset = correction[c] * OFFSET_SCALE
                if c in AXIS_GREEN:
                    offset = offset - (scales[c] / NV) * out[0][1]
                offsets[c] = offset
            waves.append(out)
        for high in range(4):
            tab = [table_rows[k + 4 * high, t] for t in range(12)]
            real = green([waves[c][high][0] for c in range(6)], tab)
            imag = green([waves[c][high][1] for c in range(6)], tab)
            for c in range(6):
                waves[c][high] = (real[c], imag[c])
        for c in range(6):
            for residue, (re, im) in enumerate(dft16_first(waves[c], k, 1)):
                back_lines[c, residue, k, 0] = re
                back_lines[c, residue, k, 1] = im

    def to_plane(k):
        ends = []
        for c in range(6):
            ends.append(
                dft4([(back_lines[c, k, n, 0], back_lines[c, k, n, 1]) for n in range(4)], 1)
            )
        for c in range(6):
            for pair in range(2):
                re, im = [], []
                for n in (2 * pair, 2 * pair + 1):
                    own = ends[c][n][1]
                    if SWAP[c] != c:
                        own = jnp.where(lane == 126, ends[SWAP[c]][n][1], own)
                    axis_value = offsets[c]
                    if c in AXIS_GREEN:
                        row = (c * 4 + n) * SLOTS
                        axis_value = (
                            axis_value + scales[c] * plane[k, row : row + SLOTS, LANES:]
                        )
                    im.append(jnp.where(lane == 127, axis_value, own))
                    re.append(ends[c][n][0])
                value = jnp.concatenate(
                    [jnp.concatenate(re, axis=0), jnp.concatenate(im, axis=0)], axis=1
                )
                high, low = split(value)
                put = slice((c * 2 + pair) * 16, (c * 2 + pair + 1) * 16)
                parts[k, 0, put, :] = high
                parts[k, 1, put, :] = low

    def to_voxels(k):
        back[k] = product(parts[k, 0], parts[k, 1], inverse)

    def update(k, step, masks, sums):
        switch, later, active = masks
        for pair in range(2):
            place = slice((k * 2 + pair) * 16, (k * 2 + pair + 1) * 16)
            strain = []
            for c in range(6):
                ended = state[0, c, place, :]
                if step is not None:
                    put = slice((c * 2 + pair) * 16, (c * 2 + pair + 1) * 16)
                    ended = ended + back[k, put, :]
                    waiting = state[1, c, place, :]
                    state[1, c, place, :] = jnp.where(switch, ended, waiting)
                    ended = jnp.where(switch, waiting, ended)
                    state[0, c, place, :] = ended
                strain.append(ended)
            shear, pressure = double_shear[0, place, :], lame[0, place, :]
            if step is not None:
                shear = active * jnp.where(later, double_shear[1, place, :], shear)
                pressure = active * jnp.where(later, lame[1, place, :], pressure)
            pressure = pressure * ((strain[0] + strain[1]) + strain[2])
            for c in range(6):
                stress = shear * strain[c]
                if c < 3:
                    stress = stress + pressure
                high, low = split(stress)
                put = slice((c * 2 + pair) * 16, (c * 2 + pair + 1) * 16)
                stresses[k, 0, put, :] = high
                stresses[k, 1, put, :] = low
                own = strain[c][:SLOTS] + strain[c][SLOTS:]
                sums[c] = own if sums[c] is None else sums[c] + own

    def to_waves(k):
        plane[k] = product(stresses[k, 0], stresses[k, 1], forward)

    def from_plane(k):
        for c in range(6):
            line = []
            for n in range(4):
                row = (c * 4 + n) * SLOTS
                re = plane[k, row : row + SLOTS, :LANES]
                im = plane[k, row : row + SLOTS, LANES:]
                if SWAP[c] != c:
                    row = (SWAP[c] * 4 + n) * SLOTS
                    im = jnp.where(lane == 126, plane[k, row : row + SLOTS, LANES:], im)
                line.append((re, im))
            for residue, (re, im) in enumerate(dft16_first(line, k, -1)):
                lines[c, residue, k, 0] = re
                lines[c, residue, k, 1] = im

    def correct(later, active, sums):
        for c in range(6):
            mean = jnp.sum(sums[c], axis=1, keepdims=True) * (1.0 / VOX)
            own = macro[0, c] if later is None else jnp.where(later, macro[1, c], macro[0, c])
            own = own * MANDEL[c] - mean
            correction[c] = own if active is None else own * active

    def wide(mask):
        mask = jnp.concatenate([mask, mask], axis=1)
        return jnp.concatenate([mask, mask], axis=0)

    def sweep(step, carry):
        step = step + 1
        switch, later = first_rows == step, first_rows <= step
        active = (step < total_rows).astype(f32)
        masks = (wide(switch), wide(later), wide(active))
        sums = [None] * 6
        for k in range(4):
            wave_part(k)
        stages = [
            to_plane,
            to_voxels,
            lambda k: update(k, step, masks, sums),
            to_waves,
            from_plane,
        ]
        for stage in stages:
            for k in range(4):
                stage(k)
        correct(later, active, sums)
        return carry

    sums = [None] * 6
    for k in range(4):
        update(k, None, (None, None, None), sums)
        to_waves(k)
    for k in range(4):
        from_plane(k)
    correct(None, None, sums)
    lax.fori_loop(0, limit, sweep, 0)

    def gather(x, sums):
        place = pl.ds(pl.multiple_of(((x & 3) * 4 + (x >> 2)) * SLOTS, SLOTS), SLOTS)
        out = []
        for half in range(2):
            strain = [state[1 - half, c, place, :] for c in range(6)]
            shear = double_shear[half, place, :]
            pressure = lame[half, place, :] * ((strain[0] + strain[1]) + strain[2])
            for c in range(6):
                stress = shear * strain[c]
                if c < 3:
                    stress = stress + pressure
                out.append(sums[6 * half + c] + (stress[:, :LANES] + stress[:, LANES:]))
                state[1 - half, c, place, :] = strain[c] * (1.0 / MANDEL[c])
        for side in range(2):
            cut = slice(side * LANES, (side + 1) * LANES)
            lanes = pl.ds(pl.multiple_of(x * PLANE + side * LANES, LANES), LANES)
            for block in range(2):
                rows_of = source[2 + block]
                for c in range(6):
                    ends = [
                        state[1 - half, c, place, cut] - macro[half, c] for half in range(2)
                    ]
                    fluctuation_out[c, block * SLOTS : (block + 1) * SLOTS, lanes] = pick(
                        *ends, rows_of
                    )
        departure(x).start()
        return tuple(out)

    def departure(x):
        lanes = pl.ds(pl.multiple_of(x * PLANE, PLANE), PLANE)
        return pltpu.make_async_copy(
            fluctuation_out.at[:, :, lanes], fluctuation_home.at[:, :, lanes], out_done.at[x]
        )

    def depart(x, carry):
        departure(x).wait()
        return carry

    for r in range(RVES):
        where_is[order[r]] = r
    for block in range(2):
        source[2 + block] = column([where_is[block * SLOTS + s] for s in range(SLOTS)])
    sums = lax.fori_loop(
        0, NV, gather, tuple(jnp.zeros((SLOTS, LANES), f32) for _ in range(12))
    )
    for half in range(2):
        for c in range(6):
            mean = jnp.sum(sums[6 * half + c], axis=1, keepdims=True)
            mean = mean * (1.0 / (VOX * MANDEL[c]))
            means[half, c] = jnp.broadcast_to(mean, (SLOTS, LANES))
    for block in range(2):
        for c in range(6):
            base = c * RVES + block * SLOTS
            rows[base : base + SLOTS, :] = pick(means[0, c], means[1, c], source[2 + block])

    stress_rows = jnp.concatenate([rows[0:96, :], jnp.zeros((32, LANES), f32)], axis=0)
    force = exact(line_tables[NV * 12 + 96 :, :], stress_rows)
    lane_of = lax.broadcasted_iota(jnp.int32, (16, LANES), 1)
    right = []
    for low in range(2):
        block = jnp.zeros((16, LANES), f32)
        for i in range(3):
            block = jnp.where(lane_of == 3 * low + i, force[16 * i : 16 * i + 16], block)
        right.append(block)
    block = jnp.zeros((16, LANES), f32)
    for c in range(6):
        block = jnp.where(lane_of == 6 + c, rows[c * RVES : (c + 1) * RVES, :], block)
    right.append(block)
    right.append(jnp.zeros((80, LANES), f32))
    target = [jnp.where((n & 1) == 0, n >> 1, -1) for n in nodes]
    target += [jnp.where((n & 1) == 1, n >> 1, -1) for n in nodes]
    target += [elem[0] * RVES + routing[r] for r in range(RVES)]
    wanted = from_scalars(target, 1, (LANES, LANES))
    taken = (lax.broadcasted_iota(jnp.int32, (LANES, LANES), 0) == wanted).astype(f32)
    sent[...] = exact(taken, jnp.concatenate(right, axis=0)).reshape(LANES, 1, LANES)
    lax.fori_loop(0, NV, depart, 0)


def solve(counts, routing, connectivity, elem, motion, fluctuation, phases, damage):
    both_planes = np.stack([split_table(table) for table in plane_tables()])
    strain_table, force_table = element_tables()
    line_tables = np.zeros((NV * 12 + 96 + 48, LANES), np.float32)
    line_tables[: NV * 12] = green_tables().reshape(NV * 12, LANES)
    line_tables[NV * 12 : NV * 12 + 96, :48] = strain_table
    line_tables[NV * 12 + 96 :, :96] = force_table
    smem = pl.BlockSpec(memory_space=pltpu.SMEM)
    vmem = pl.BlockSpec(memory_space=pltpu.VMEM)
    hbm = pl.BlockSpec(memory_space=pltpu.HBM)
    f32 = jnp.float32
    scratch = [
        pltpu.SMEM((RVES,), jnp.int32),
        pltpu.SMEM((RVES,), jnp.int32),
        pltpu.VMEM((2, 6, ROWS, PLANE), f32),
        pltpu.VMEM((2, ROWS, PLANE), f32),
        pltpu.VMEM((2, ROWS, PLANE), f32),
        pltpu.VMEM((2, 6, SLOTS, LANES), f32),
        pltpu.VMEM((96, LANES), f32),
        pltpu.VMEM((4, 2, 192, PLANE), jnp.bfloat16),
        pltpu.VMEM((4, 2, 192, PLANE), jnp.bfloat16),
        pltpu.VMEM((4, 192, PLANE), f32),
        pltpu.VMEM((4, 192, PLANE), f32),
        pltpu.VMEM((6, 4, 4, 2, SLOTS, LANES), f32),
        pltpu.VMEM((6, 4, 4, 2, SLOTS, LANES), f32),
        pltpu.VMEM((6, SLOTS, LANES), f32),
        pltpu.VMEM((6, SLOTS, LANES), f32),
        pltpu.VMEM((NV, 12, SLOTS, LANES), f32),
        pltpu.VMEM((2, 6, SLOTS, LANES), f32),
        pltpu.VMEM((4, SLOTS, LANES), jnp.int32),
        pltpu.SMEM((RVES,), jnp.int32),
        pltpu.VMEM((6, RVES, VOX), f32),
        pltpu.VMEM((RVES, VOX), jnp.int32),
        pltpu.VMEM((RVES, VOX), f32),
        pltpu.VMEM((2, 768, PLANE), jnp.bfloat16),
        pltpu.VMEM((NV * 12 + 96 + 48, LANES), f32),
        pltpu.SemaphoreType.DMA((10,)),
        pltpu.SemaphoreType.DMA((NV,)),
    ]
    return pl.pallas_call(
        pool_kernel,
        out_shape=(
            jax.ShapeDtypeStruct((6, RVES, VOX), f32),
            jax.ShapeDtypeStruct((LANES, 1, LANES), f32),
        ),
        in_specs=[smem] * 4 + [vmem] + [hbm] * 5,
        out_specs=(hbm, vmem),
        scratch_shapes=scratch,
        compiler_params=pltpu.CompilerParams(vmem_limit_bytes=56 * 1024 * 1024),
        name="solve_rves",
    )(
        counts,
        routing,
        connectivity,
        elem,
        motion,
        fluctuation,
        phases,
        damage,
        jnp.asarray(both_planes),
        jnp.asarray(line_tables),
    )


def exchange(rows):
    return lax.all_to_all(rows, ("elem", "rve"), split_axis=0, concat_axis=0, tiled=True)


def shards(
    displacement,
    connectivity,
    fluctuation,
    phases,
    damage,
    iteration_counts,
    routing,
    external_force,
):
    devices = LANES
    own = jnp.pad(displacement.T.reshape(1, 1, 6), ((0, 0), (0, 0), (0, LANES - 6)))
    motion = exchange(jnp.broadcast_to(own, (devices, 1, LANES)))
    elem = lax.axis_index("elem")
    fluctuation_out, sent = solve(
        iteration_counts,
        routing,
        connectivity,
        elem.astype(jnp.int32).reshape(1),
        motion,
        jnp.transpose(fluctuation, (1, 0, 2)),
        phases,
        damage,
    )
    fluctuation_out = jnp.transpose(fluctuation_out, (1, 0, 2))
    received = exchange(sent)[:, 0, :]
    residual_force = jnp.sum(received[:, :6], axis=0).reshape(2, 3).T - external_force
    pool_stress = lax.dynamic_slice(received, (elem * RVES, 6), (RVES, 6))
    return (residual_force, fluctuation_out, pool_stress)


def solution(mesh):
    both = ("elem", "rve")
    return jax.shard_map(
        shards,
        mesh=mesh,
        in_specs=(
            P(None, both),
            P(None, both),
            P(both, None, None),
            P(both, None),
            P(both, None),
            P(both),
            P(both),
            P(None, both),
        ),
        out_specs=(P(None, both), P(both, None, None), P(both, None)),
        check_vma=False,
    )
```

```python
import math

import jax
import jax.numpy as jnp
import ml_dtypes
import numpy as np
from jax import lax
from jax.experimental import pallas as pl
from jax.experimental.pallas import tpu as pltpu
from jax.sharding import PartitionSpec as P

NV = 16
PLANE = NV * NV
VOX = NV**3
LANES = 128
SLOTS = 8
RVES = 16
ROWS = NV * SLOTS
MU_PHASE = (0.1, 0.4, 2.0)
LAM_PHASE = (0.15, 0.6, 1.0)
mu_ref = 1.053
lam_ref = 0.5295
component_pairs = ((0, 0), (1, 1), (2, 2), (1, 2), (0, 2), (0, 1))
component_index = {tuple(sorted(pair)): c for c, pair in enumerate(component_pairs)}
SQRT2 = math.sqrt(2.0)
MANDEL = (1.0, 1.0, 1.0, SQRT2, SQRT2, SQRT2)
SWAP = (0, 2, 1, 3, 5, 4)
NORMAL_SCALE = (lam_ref + mu_ref) / (lam_ref + 2.0 * mu_ref)
GREEN_SCALE = 2.0 * NORMAL_SCALE
INVERSE_SCALE = -2.0 / (mu_ref * VOX) / GREEN_SCALE
AXIS_SCALE = -2.0 / PLANE / INVERSE_SCALE
OFFSET_SCALE = 2.0 / INVERSE_SCALE
AXIS_GREEN = {0: 1.0 / (lam_ref + 2.0 * mu_ref), 4: 0.5 / mu_ref, 5: 0.5 / mu_ref}
HIGHEST = lax.Precision.HIGHEST


def shape_gradients():
    lower = 0.5 - 0.5 / math.sqrt(3.0)
    upper = 0.5 + 0.5 / math.sqrt(3.0)
    table = np.zeros((8, 8, 3))
    for corner in range(8):
        bits = (corner >> 2 & 1, corner >> 1 & 1, corner & 1)
        for point in range(8):
            coords = [upper if point >> shift & 1 else lower for shift in (2, 1, 0)]
            factors = [c if b else 1.0 - c for c, b in zip(coords, bits)]
            for axis in range(3):
                entry = 1.0 if bits[axis] else -1.0
                for other in range(3):
                    if other != axis:
                        entry *= factors[other]
                table[corner, point, axis] = entry
    return table


def element_tables():
    gradient = shape_gradients()
    strain = np.zeros((6, RVES, 3, 16))
    force = np.zeros((3, 16, 6, RVES))
    for r in range(RVES):
        e, q = divmod(r, 8)
        for a in range(8):
            j = 2 * a + e
            for c, (k, h) in enumerate(component_pairs):
                strain[c, r, k, j] += 0.5 * gradient[a, q, h]
                strain[c, r, h, j] += 0.5 * gradient[a, q, k]
            for i in range(3):
                for h in range(3):
                    force[i, j, component_index[tuple(sorted((i, h)))], r] += (
                        0.125 * gradient[a, q, h]
                    )
    return strain.reshape(96, 48), force.reshape(48, 96)


def wave(m):
    return m if m < NV // 2 else m - NV


def lane_waves():
    chosen, seen = [], set()
    for ky in range(NV):
        for kz in range(NV):
            partner = (-ky % NV, -kz % NV)
            if (ky, kz) == partner or (ky, kz) in seen:
                continue
            seen.update(((ky, kz), partner))
            chosen.append((ky, kz))
    return chosen


def plane_tables():
    y, z = np.divmod(np.arange(PLANE), NV)
    forward = np.zeros((PLANE, 2 * LANES))
    for lane, (ky, kz) in enumerate(lane_waves()):
        angle = 2.0 * np.pi / NV * ((ky * y + kz * z) % NV)
        forward[:, lane] = np.cos(angle)
        forward[:, LANES + lane] = -np.sin(angle)
    forward[:, 126] = 1.0 - 2.0 * (y % 2)
    forward[:, LANES + 126] = 1.0 - 2.0 * (z % 2)
    forward[:, 127] = 1.0 - 2.0 * ((y + z) % 2)
    forward[:, LANES + 127] = 1.0
    inverse = forward.T.copy()
    inverse[[126, 127, LANES + 126, LANES + 127]] *= 0.5
    return forward, inverse * INVERSE_SCALE


def split_table(table):
    high = table.astype(ml_dtypes.bfloat16)
    low = (table - high.astype(np.float64)).astype(ml_dtypes.bfloat16)
    return np.concatenate([high, low], axis=0)


def green_tables():
    waves = lane_waves() + [(8, 0), (8, 8)]
    out = np.zeros((NV, 12, LANES))
    for kx in range(NV):
        for lane, (ky, kz) in enumerate(waves):
            index = (kx, ky, kz)
            m = np.array([wave(v) for v in index], float)
            back = np.array([wave(-v % NV) for v in index], float)
            length = np.linalg.norm(m)
            if length == 0:
                continue
            n, b = m / length, back / length
            square = n * n
            pair = lambda k, h: 0.5 * (n[k] * n[h] + b[k] * b[h])
            p = [pair(1, 2), pair(0, 2), pair(0, 1)]
            out[kx, 0:3, lane] = square
            out[kx, 3:6, lane] = [v / SQRT2 for v in p]
            for o in range(3):
                k, h = [axis for axis in range(3) if axis != o]
                out[kx, 6 + o, lane] = (
                    0.5 * (square[k] + square[h])
                    - 2.0 * NORMAL_SCALE * square[k] * square[h]
                )
                out[kx, 9 + o, lane] = p[o] * (0.5 - 2.0 * NORMAL_SCALE * square[o])
    return out * GREEN_SCALE


def twiddle(re, im, power, sign):
    power %= 16
    if power == 0:
        return re, im
    if power == 4:
        return (im, -re) if sign < 0 else (-im, re)
    angle = 2.0 * math.pi * power / 16.0
    c, s = math.cos(angle), sign * math.sin(angle)
    if power % 4 == 2:
        root = math.sqrt(0.5)
        cs, ss = math.copysign(1.0, c), math.copysign(1.0, s)
        a = re if cs > 0 else -re
        b = im if cs > 0 else -im
        if cs * ss > 0:
            real, imag = (re - im), (re + im)
        else:
            real, imag = (re + im), (im - re)
        return real * (cs * root), imag * (cs * root)
    return re * c - im * s, re * s + im * c


def dft4(v, sign):
    (ar, ai), (br, bi), (cr, ci), (dr, di) = v
    sr, si, tr, ti = ar + cr, ai + ci, ar - cr, ai - ci
    ur, ui, wr, wi = br + dr, bi + di, br - dr, bi - di
    if sign < 0:
        return [
            (sr + ur, si + ui),
            (tr + wi, ti - wr),
            (sr - ur, si - ui),
            (tr - wi, ti + wr),
        ]
    return [
        (sr + ur, si + ui),
        (tr - wi, ti + wr),
        (sr - ur, si - ui),
        (tr + wi, ti - wr),
    ]


def dft16_first(values, first, sign):
    inner = dft4(values, sign)
    return [twiddle(*inner[k], first * k, sign) for k in range(4)]


def green(t, tab):
    xyz = [tab[a] * t[a] for a in range(3)]
    d = (xyz[0] + xyz[1]) + xyz[2]
    o = [tab[3 + a] * t[3 + a] for a in range(3)]
    sums = [o[1] + o[2], o[0] + o[2], o[0] + o[1]]
    s = sums[0] + o[0]
    m = 0.5 * d + s
    out = [(xyz[a] + sums[a]) - tab[a] * m for a in range(3)]
    for a in range(3):
        k, h = [axis for axis in range(3) if axis != a]
        value = tab[3 + a] * ((t[k] + t[h]) - d) + tab[6 + a] * t[3 + a]
        value = value + (tab[9 + h] * t[3 + k] + tab[9 + k] * t[3 + h])
        out.append(value)
    return out


def split(value):
    high = value.astype(jnp.bfloat16)
    low = (value - high.astype(jnp.float32)).astype(jnp.bfloat16)
    return high, low


def product(high, low, table_ref):
    f32 = jnp.float32
    rows = high.shape[0]
    both = jnp.concatenate([high, low], axis=0)
    both = jnp.dot(both, table_ref[:PLANE], preferred_element_type=f32)
    rest = jnp.dot(high, table_ref[PLANE:], preferred_element_type=f32)
    return (both[:rows] + both[rows:]) + rest


def exact(left, right):
    return jnp.dot(left, right, precision=HIGHEST, preferred_element_type=jnp.float32)


def from_scalars(scalars, axis, shape):
    place = lax.broadcasted_iota(jnp.int32, shape, axis)
    out = jnp.full(shape, -1, jnp.int32)
    for index, value in enumerate(scalars):
        out = jnp.where(place == index, value, out)
    return out


def column(values):
    return from_scalars(values, 0, (SLOTS, LANES))


def pick(low, high, rows_of):
    place = rows_of & 7
    low = jnp.take_along_axis(low, place, axis=0, mode="promise_in_bounds")
    high = jnp.take_along_axis(high, place, axis=0, mode="promise_in_bounds")
    return jnp.where(rows_of >= SLOTS, high, low)


def prepare_kernel(
    counts_in,
    fluctuation_in,
    phases_in,
    damage_in,
    start_home,
    places_home,
    start,
    places,
    order,
    sorted_counts,
    where_is,
    counts,
    fluctuation,
    phases,
    damage,
    in_done,
    out_done,
):
    arrivals = [
        pltpu.make_async_copy(source, target, in_done.at[n])
        for n, (source, target) in enumerate(
            [(counts_in, counts), (phases_in, phases), (damage_in, damage)]
            + [(fluctuation_in.at[c], fluctuation.at[c]) for c in range(6)]
        )
    ]
    for arrival in arrivals:
        arrival.start()
    arrivals[0].wait()
    values = [counts[r] for r in range(RVES)]
    for r in range(RVES):
        rank = jnp.int32(0)
        for j in range(RVES):
            if j != r:
                ahead = values[j] >= values[r] if j < r else values[j] > values[r]
                rank = rank + ahead.astype(jnp.int32)
        place = jnp.where(rank < SLOTS, rank, RVES + SLOTS - 1 - rank)
        order[place] = r
        sorted_counts[place] = values[r]
        where_is[r] = place
    for half in range(2):
        places[half] = column([order[half * SLOTS + s] for s in range(SLOTS)])
        places[2 + half] = column([where_is[half * SLOTS + s] for s in range(SLOTS)])
    places[4] = column([sorted_counts[s] for s in range(SLOTS)])
    places[5] = column([sorted_counts[s] + sorted_counts[SLOTS + s] for s in range(SLOTS)])
    for arrival in arrivals[1:]:
        arrival.wait()

    departures = [pltpu.make_async_copy(places, places_home, out_done.at[4])]
    departures[0].start()

    def load(n, k):
        x = 4 * n + k
        for side in range(2):
            lanes = pl.ds(pl.multiple_of(x * PLANE + side * LANES, LANES), LANES)
            place = pl.ds(pl.multiple_of((k * 4 + n) * SLOTS, SLOTS), SLOTS)
            cut = slice(side * LANES, (side + 1) * LANES)
            phase = phases[:, lanes]
            soft = 1.0 - damage[:, lanes]
            soft = soft * soft + 0.05
            shear = soft * jnp.where(
                phase == 0,
                2.0 * MU_PHASE[0],
                jnp.where(phase == 1, 2.0 * MU_PHASE[1], 2.0 * MU_PHASE[2]),
            )
            second = soft * jnp.where(
                phase == 0, LAM_PHASE[0], jnp.where(phase == 1, LAM_PHASE[1], LAM_PHASE[2])
            )
            for half in range(2):
                rows_of = places[half]
                start[half, 6, place, cut] = pick(shear[:SLOTS], shear[SLOTS:], rows_of)
                start[half, 7, place, cut] = pick(second[:SLOTS], second[SLOTS:], rows_of)
                for c in range(6):
                    start[half, c, place, cut] = pick(
                        fluctuation[c, :SLOTS, lanes], fluctuation[c, SLOTS:, lanes], rows_of
                    )
        return k

    for k in range(4):
        lax.fori_loop(0, 4, load, k)
        part = pl.ds(k * 32, 32)
        departures.append(
            pltpu.make_async_copy(start.at[:, :, part], start_home.at[:, :, part], out_done.at[k])
        )
        departures[-1].start()
    for departure in departures:
        departure.wait()


def finish_kernel(
    state_in, macro_in, places_in, fluctuation_home, state, macro, places, fluctuation, in_done, out_done
):
    arrivals = [
        pltpu.make_async_copy(macro_in, macro, in_done.at[4]),
        pltpu.make_async_copy(places_in, places, in_done.at[5]),
    ]
    for k in range(4):
        part = pl.ds(k * 32, 32)
        arrivals.append(
            pltpu.make_async_copy(
                state_in.at[:, :, part], state.at[:, :, part], in_done.at[k]
            )
        )
    for arrival in arrivals:
        arrival.start()

    def departure(x):
        lanes = pl.ds(pl.multiple_of(x * PLANE, PLANE), PLANE)
        return pltpu.make_async_copy(
            fluctuation.at[:, :, lanes], fluctuation_home.at[:, :, lanes], out_done.at[x]
        )

    def gather(n, k):
        x = 4 * n + k
        place = pl.ds(pl.multiple_of((k * 4 + n) * SLOTS, SLOTS), SLOTS)
        for side in range(2):
            cut = slice(side * LANES, (side + 1) * LANES)
            lanes = pl.ds(pl.multiple_of(x * PLANE + side * LANES, LANES), LANES)
            for c in range(6):
                ends = [
                    state[1 - half, c, place, cut] * (1.0 / MANDEL[c]) - macro[half, c]
                    for half in range(2)
                ]
                for block in range(2):
                    fluctuation[c, block * SLOTS : (block + 1) * SLOTS, lanes] = pick(
                        *ends, places[2 + block]
                    )
        departure(x).start()
        return k

    def depart(x, carry):
        departure(x).wait()
        return carry

    for arrival in arrivals[:2]:
        arrival.wait()
    for k in range(4):
        arrivals[2 + k].wait()
        lax.fori_loop(0, 4, gather, k)
    lax.fori_loop(0, NV, depart, 0)


def collect_kernel(
    elem, received, external_force, residual_home, pool_home, residual_force, pool_stress, out_done
):
    total = jnp.sum(received[...].reshape(LANES, LANES), axis=0, keepdims=True)
    node = lax.broadcasted_iota(jnp.int32, (2, 3), 0)
    residual_force[...] = (
        jnp.where(node == 0, total[:, 0:3], total[:, 3:6]) - external_force[...]
    )
    own = pl.ds(pl.multiple_of(elem[0] * RVES, RVES), RVES)
    pool_stress[...] = received[own].reshape(RVES, LANES).T[6:12, :]
    departures = [
        pltpu.make_async_copy(residual_force, residual_home, out_done.at[0]),
        pltpu.make_async_copy(pool_stress, pool_home, out_done.at[1]),
    ]
    for departure in departures:
        departure.start()
    for departure in departures:
        departure.wait()


def sweep_kernel(
    elem,
    motion_in,
    routing_in,
    connectivity_in,
    places_in,
    line_tables_in,
    start_in,
    plane_tables_in,
    state,
    macro,
    sent,
    motion,
    routing,
    connectivity,
    places,
    line_tables,
    start,
    plane_tables,
    table_rows,
    rows,
    parts,
    stresses,
    plane,
    back,
    lines,
    back_lines,
    correction,
    offsets,
    means,
    in_done,
):
    f32 = jnp.float32
    arrivals = [
        pltpu.make_async_copy(source, target, in_done.at[n])
        for n, (source, target) in enumerate(
            [
                (motion_in, motion),
                (routing_in, routing),
                (connectivity_in, connectivity),
                (places_in, places),
                (line_tables_in, line_tables),
                (start_in.at[0], start.at[0]),
                (start_in.at[1], start.at[1]),
                (plane_tables_in, plane_tables),
            ]
        )
    ]
    for arrival in arrivals:
        arrival.start()
    for arrival in arrivals[:5]:
        arrival.wait()
    forward, inverse = plane_tables.at[0], plane_tables.at[1]
    nodes = [connectivity[e, a] for a in range(8) for e in range(2)]
    node_rows = from_scalars(nodes, 0, (16, LANES))
    holder = (lax.broadcasted_iota(jnp.int32, (16, LANES), 1) == (node_rows >> 1)).astype(f32)
    corner = exact(holder, motion[...].reshape(LANES, LANES))
    odd = (node_rows & 1) == 1
    moved = [
        jnp.where(
            odd,
            jnp.broadcast_to(corner[:, 3 + i : 4 + i], (16, LANES)),
            jnp.broadcast_to(corner[:, i : i + 1], (16, LANES)),
        )
        for i in range(3)
    ]
    moved = jnp.concatenate(moved + [jnp.zeros((LANES - 48, LANES), f32)], axis=0)
    for row in range(NV * 12):
        table_rows[row] = jnp.broadcast_to(line_tables[row : row + 1, :], (SLOTS, LANES))
    rows[0:96, :] = exact(line_tables[NV * 12 : NV * 12 + 96, :], moved)
    for half in range(2):
        for c in range(6):
            low = rows[c * RVES : c * RVES + SLOTS, :]
            high = rows[c * RVES + SLOTS : (c + 1) * RVES, :]
            macro[half, c] = pick(low, high, places[half])

    lane = lax.broadcasted_iota(jnp.int32, (SLOTS, LANES), 1)
    first_rows, total_rows = places[4], places[5]
    limit = jnp.max(total_rows.astype(f32)).astype(jnp.int32)

    scales = [AXIS_SCALE * AXIS_GREEN.get(c, 0.0) for c in range(6)]

    def wave_part(k):
        waves = []
        for c in range(6):
            out = dft4([(lines[c, k, first, 0], lines[c, k, first, 1]) for first in range(4)], -1)
            if k == 0:
                offset = correction[c] * OFFSET_SCALE
                if c in AXIS_GREEN:
                    offset = offset - (scales[c] / NV) * out[0][1]
                offsets[c] = offset
            waves.append(out)
        for high in range(4):
            tab = [table_rows[(k + 4 * high) * 12 + t] for t in range(12)]
            real = green([waves[c][high][0] for c in range(6)], tab)
            imag = green([waves[c][high][1] for c in range(6)], tab)
            for c in range(6):
                waves[c][high] = (real[c], imag[c])
        for c in range(6):
            for residue, (re, im) in enumerate(dft16_first(waves[c], k, 1)):
                back_lines[c, residue, k, 0] = re
                back_lines[c, residue, k, 1] = im

    def to_plane(k):
        ends = []
        for c in range(6):
            ends.append(
                dft4([(back_lines[c, k, n, 0], back_lines[c, k, n, 1]) for n in range(4)], 1)
            )
        for c in range(6):
            for pair in range(2):
                re, im = [], []
                for n in (2 * pair, 2 * pair + 1):
                    own = ends[c][n][1]
                    if SWAP[c] != c:
                        own = jnp.where(lane == 126, ends[SWAP[c]][n][1], own)
                    axis_value = offsets[c]
                    if c in AXIS_GREEN:
                        row = (c * 4 + n) * SLOTS
                        axis_value = (
                            axis_value + scales[c] * plane[k, row : row + SLOTS, LANES:]
                        )
                    im.append(jnp.where(lane == 127, axis_value, own))
                    re.append(ends[c][n][0])
                value = jnp.concatenate(
                    [jnp.concatenate(re, axis=0), jnp.concatenate(im, axis=0)], axis=1
                )
                high, low = split(value)
                put = slice((c * 2 + pair) * 16, (c * 2 + pair + 1) * 16)
                parts[k, 0, put, :] = high
                parts[k, 1, put, :] = low

    def to_voxels(k):
        back[k] = product(parts[k, 0], parts[k, 1], inverse)

    def update(k, step, masks, sums):
        switch, later, active = masks
        for pair in range(2):
            place = slice((k * 2 + pair) * 16, (k * 2 + pair + 1) * 16)
            strain = []
            for c in range(6):
                if step is None:
                    for half in (1, 0):
                        own = jnp.concatenate([macro[half, c]] * 2, axis=0)
                        own = jnp.concatenate([own, own], axis=1)
                        ended = (start[half, c, place, :] + own) * MANDEL[c]
                        state[half, c, place, :] = ended
                else:
                    ended = state[0, c, place, :]
                    put = slice((c * 2 + pair) * 16, (c * 2 + pair + 1) * 16)
                    ended = ended + back[k, put, :]
                    waiting = state[1, c, place, :]
                    pltpu.store(state.at[1, c, place, :], ended, mask=switch)
                    ended = jnp.where(switch, waiting, ended)
                    state[0, c, place, :] = ended
                strain.append(ended)
            shear, pressure = start[0, 6, place, :], start[0, 7, place, :]
            if step is not None:
                shear = active * jnp.where(later, start[1, 6, place, :], shear)
                pressure = active * jnp.where(later, start[1, 7, place, :], pressure)
            pressure = pressure * ((strain[0] + strain[1]) + strain[2])
            for c in range(6):
                stress = shear * strain[c]
                if c < 3:
                    stress = stress + pressure
                high, low = split(stress)
                put = slice((c * 2 + pair) * 16, (c * 2 + pair + 1) * 16)
                stresses[k, 0, put, :] = high
                stresses[k, 1, put, :] = low
                own = strain[c][:SLOTS] + strain[c][SLOTS:]
                sums[c] = own if sums[c] is None else sums[c] + own

    def to_waves(k):
        plane[k] = product(stresses[k, 0], stresses[k, 1], forward)

    def from_plane(k):
        for c in range(6):
            line = []
            for n in range(4):
                row = (c * 4 + n) * SLOTS
                re = plane[k, row : row + SLOTS, :LANES]
                im = plane[k, row : row + SLOTS, LANES:]
                if SWAP[c] != c:
                    row = (SWAP[c] * 4 + n) * SLOTS
                    im = jnp.where(lane == 126, plane[k, row : row + SLOTS, LANES:], im)
                line.append((re, im))
            for residue, (re, im) in enumerate(dft16_first(line, k, -1)):
                lines[c, residue, k, 0] = re
                lines[c, residue, k, 1] = im

    def correct(later, active, sums):
        for c in range(6):
            mean = jnp.sum(sums[c], axis=1, keepdims=True) * (1.0 / VOX)
            own = macro[0, c] if later is None else jnp.where(later, macro[1, c], macro[0, c])
            own = own * MANDEL[c] - mean
            correction[c] = own if active is None else own * active

    def wide(mask):
        mask = jnp.concatenate([mask, mask], axis=1)
        return jnp.concatenate([mask, mask], axis=0)

    def sweep(step, carry):
        step = step + 1
        switch, later = first_rows == step, first_rows <= step
        active = (step < total_rows).astype(f32)
        masks = (wide(switch), wide(later), wide(active))
        sums = [None] * 6
        for k in range(4):
            wave_part(k)
        stages = [
            to_plane,
            to_voxels,
            lambda k: update(k, step, masks, sums),
            to_waves,
            from_plane,
        ]
        for stage in stages:
            for k in range(4):
                stage(k)
        correct(later, active, sums)
        return carry

    for arrival in arrivals[5:]:
        arrival.wait()
    sums = [None] * 6
    for k in range(4):
        update(k, None, (None, None, None), sums)
        to_waves(k)
    for k in range(4):
        from_plane(k)
    correct(None, None, sums)
    lax.fori_loop(0, limit, sweep, 0)

    def gather(x, sums):
        place = pl.ds(pl.multiple_of(x * 2 * SLOTS, 2 * SLOTS), 2 * SLOTS)
        out = []
        for half in range(2):
            strain = [state[1 - half, c, place, :] for c in range(6)]
            shear = start[half, 6, place, :]
            pressure = start[half, 7, place, :] * ((strain[0] + strain[1]) + strain[2])
            for c in range(6):
                stress = shear * strain[c]
                if c < 3:
                    stress = stress + pressure
                stress = stress[:SLOTS] + stress[SLOTS:]
                out.append(sums[6 * half + c] + (stress[:, :LANES] + stress[:, LANES:]))
        return tuple(out)

    sums = lax.fori_loop(
        0, NV // 2, gather, tuple(jnp.zeros((SLOTS, LANES), f32) for _ in range(12))
    )
    for half in range(2):
        for c in range(6):
            mean = jnp.sum(sums[6 * half + c], axis=1, keepdims=True)
            mean = mean * (1.0 / (VOX * MANDEL[c]))
            means[half, c] = jnp.broadcast_to(mean, (SLOTS, LANES))
    for block in range(2):
        for c in range(6):
            base = c * RVES + block * SLOTS
            rows[base : base + SLOTS, :] = pick(means[0, c], means[1, c], places[2 + block])

    stress_rows = jnp.concatenate([rows[0:96, :], jnp.zeros((32, LANES), f32)], axis=0)
    force = exact(line_tables[NV * 12 + 96 :, :], stress_rows)
    lane_of = lax.broadcasted_iota(jnp.int32, (16, LANES), 1)
    right = []
    for low in range(2):
        block = jnp.zeros((16, LANES), f32)
        for i in range(3):
            block = jnp.where(lane_of == 3 * low + i, force[16 * i : 16 * i + 16], block)
        right.append(block)
    block = jnp.zeros((16, LANES), f32)
    for c in range(6):
        block = jnp.where(lane_of == 6 + c, rows[c * RVES : (c + 1) * RVES, :], block)
    right.append(block)
    right.append(jnp.zeros((80, LANES), f32))
    target = [jnp.where((n & 1) == 0, n >> 1, -1) for n in nodes]
    target += [jnp.where((n & 1) == 1, n >> 1, -1) for n in nodes]
    target += [elem[0] * RVES + routing[r] for r in range(RVES)]
    wanted = from_scalars(target, 1, (LANES, LANES))
    taken = (lax.broadcasted_iota(jnp.int32, (LANES, LANES), 0) == wanted).astype(f32)
    sent[...] = exact(taken, jnp.concatenate(right, axis=0)).reshape(LANES, 1, LANES)


def tables():
    plane_table = np.stack([split_table(table) for table in plane_tables()])
    strain_table, force_table = element_tables()
    line_table = np.zeros((NV * 12 + 96 + 48, LANES), np.float32)
    line_table[: NV * 12] = green_tables().reshape(NV * 12, LANES)
    line_table[NV * 12 : NV * 12 + 96, :48] = strain_table
    line_table[NV * 12 + 96 :, :96] = force_table
    return plane_table, line_table


SMEM = pl.BlockSpec(memory_space=pltpu.SMEM)
VMEM = pl.BlockSpec(memory_space=pltpu.VMEM)
HBM = pl.BlockSpec(memory_space=pltpu.HBM)
VMEM_MIB = 40
SOLVE_MIB = 54
PREPARE_MIB = 61
FINISH_MIB = 61
PARAMS = pltpu.CompilerParams(vmem_limit_bytes=VMEM_MIB * 1024 * 1024)


def of(shape, kind=jnp.float32):
    return jax.ShapeDtypeStruct(shape, kind)


def prepare(counts, fluctuation, phases, damage):
    f32 = jnp.float32
    return pl.pallas_call(
        prepare_kernel,
        out_shape=(
            of((2, 8, ROWS, PLANE)),
            of((6, SLOTS, LANES), jnp.int32),
        ),
        in_specs=[HBM] * 4,
        out_specs=(HBM, HBM),
        scratch_shapes=[
            pltpu.VMEM((2, 8, ROWS, PLANE), f32),
            pltpu.VMEM((6, SLOTS, LANES), jnp.int32),
            pltpu.SMEM((RVES,), jnp.int32),
            pltpu.SMEM((RVES,), jnp.int32),
            pltpu.SMEM((RVES,), jnp.int32),
            pltpu.SMEM((RVES,), jnp.int32),
            pltpu.VMEM((6, RVES, VOX), f32),
            pltpu.VMEM((RVES, VOX), jnp.int32),
            pltpu.VMEM((RVES, VOX), f32),
            pltpu.SemaphoreType.DMA((9,)),
            pltpu.SemaphoreType.DMA((5,)),
        ],
        cost_estimate=pl.CostEstimate(
            flops=8_000_000, bytes_accessed=8_000_000, transcendentals=0
        ),
        compiler_params=pltpu.CompilerParams(vmem_limit_bytes=PREPARE_MIB * 1024 * 1024),
        name="prepare_rves",
    )(counts, fluctuation, phases, damage)


def solve(routing, connectivity, elem, motion, prepared):
    f32 = jnp.float32
    plane_table, line_table = tables()
    return pl.pallas_call(
        sweep_kernel,
        out_shape=(of((2, 6, ROWS, PLANE)), of((2, 6, SLOTS, LANES)), of((LANES, 1, LANES))),
        in_specs=[SMEM] + [HBM] * 7,
        out_specs=(VMEM,) * 3,
        scratch_shapes=[
            pltpu.VMEM((LANES, 1, LANES), f32),
            pltpu.SMEM((RVES,), jnp.int32),
            pltpu.SMEM((2, 8), jnp.int32),
            pltpu.VMEM((6, SLOTS, LANES), jnp.int32),
            pltpu.VMEM(line_table.shape, f32),
            pltpu.VMEM((2, 8, ROWS, PLANE), f32),
            pltpu.VMEM(plane_table.shape, jnp.bfloat16),
            pltpu.VMEM((NV * 12, SLOTS, LANES), f32),
            pltpu.VMEM((96, LANES), f32),
            pltpu.VMEM((4, 2, 192, PLANE), jnp.bfloat16),
            pltpu.VMEM((4, 2, 192, PLANE), jnp.bfloat16),
            pltpu.VMEM((4, 192, PLANE), f32),
            pltpu.VMEM((4, 192, PLANE), f32),
            pltpu.VMEM((6, 4, 4, 2, SLOTS, LANES), f32),
            pltpu.VMEM((6, 4, 4, 2, SLOTS, LANES), f32),
            pltpu.VMEM((6, SLOTS, LANES), f32),
            pltpu.VMEM((6, SLOTS, LANES), f32),
            pltpu.VMEM((2, 6, SLOTS, LANES), f32),
            pltpu.SemaphoreType.DMA((8,)),
        ],
        compiler_params=pltpu.CompilerParams(vmem_limit_bytes=SOLVE_MIB * 1024 * 1024),
        name="solve_rves",
    )(
        elem,
        motion,
        routing,
        connectivity,
        prepared[1],
        jnp.asarray(line_table),
        prepared[0],
        jnp.asarray(plane_table),
    )


def finish(state, macro, places):
    return pl.pallas_call(
        finish_kernel,
        out_shape=of((6, RVES, VOX)),
        in_specs=[HBM] * 3,
        out_specs=HBM,
        scratch_shapes=[
            pltpu.VMEM((2, 6, ROWS, PLANE), jnp.float32),
            pltpu.VMEM((2, 6, SLOTS, LANES), jnp.float32),
            pltpu.VMEM((6, SLOTS, LANES), jnp.int32),
            pltpu.VMEM((6, RVES, VOX), jnp.float32),
            pltpu.SemaphoreType.DMA((6,)),
            pltpu.SemaphoreType.DMA((NV,)),
        ],
        cost_estimate=pl.CostEstimate(
            flops=4_000_000, bytes_accessed=4_000_000, transcendentals=0
        ),
        compiler_params=pltpu.CompilerParams(vmem_limit_bytes=FINISH_MIB * 1024 * 1024),
        name="finish_rves",
    )(state, macro, places)


def exchange(rows):
    return lax.all_to_all(rows, ("elem", "rve"), split_axis=0, concat_axis=0, tiled=True)


def shards(
    displacement,
    connectivity,
    fluctuation,
    phases,
    damage,
    iteration_counts,
    routing,
    external_force,
):
    own = jnp.pad(displacement.T.reshape(1, 1, 6), ((0, 0), (0, 0), (0, LANES - 6)))
    own = jnp.broadcast_to(own, (LANES, 1, LANES))
    motion = exchange(own)
    elem = lax.axis_index("elem").astype(jnp.int32).reshape(1)
    prepared = prepare(
        iteration_counts, jnp.transpose(fluctuation, (1, 0, 2)), phases, damage
    )
    state, macro, sent = solve(routing, connectivity.T, elem, motion, prepared)
    received = exchange(sent)
    fluctuation_out = jnp.transpose(finish(state, macro, prepared[1]), (1, 0, 2))
    residual_force, pool_stress = pl.pallas_call(
        collect_kernel,
        out_shape=(of((2, 3)), of((6, RVES))),
        in_specs=[SMEM, VMEM, VMEM],
        out_specs=(HBM, HBM),
        scratch_shapes=[
            pltpu.VMEM((2, 3), jnp.float32),
            pltpu.VMEM((6, RVES), jnp.float32),
            pltpu.SemaphoreType.DMA((2,)),
        ],
        compiler_params=PARAMS,
        name="collect_results",
    )(elem, received, external_force.T)
    return (residual_force.T, fluctuation_out, pool_stress.T)


def solution(mesh):
    both = ("elem", "rve")
    return jax.shard_map(
        shards,
        mesh=mesh,
        in_specs=(
            P(None, both),
            P(None, both),
            P(both, None, None),
            P(both, None),
            P(both, None),
            P(both),
            P(both),
            P(None, both),
        ),
        out_specs=(P(None, both), P(both, None, None), P(both, None)),
        check_vma=False,
    )
```

```python
import math

import jax
import jax.numpy as jnp
import ml_dtypes
import numpy as np
from jax import lax
from jax.experimental import pallas as pl
from jax.experimental.pallas import tpu as pltpu
from jax.sharding import PartitionSpec as P

NV = 16
PLANE = NV * NV
VOX = NV**3
LANES = 128
SLOTS = 8
RVES = 16
ROWS = NV * SLOTS
MU_PHASE = (0.1, 0.4, 2.0)
LAM_PHASE = (0.15, 0.6, 1.0)
mu_ref = 1.053
lam_ref = 0.5295
component_pairs = ((0, 0), (1, 1), (2, 2), (1, 2), (0, 2), (0, 1))
component_index = {tuple(sorted(pair)): c for c, pair in enumerate(component_pairs)}
SQRT2 = math.sqrt(2.0)
MANDEL = (1.0, 1.0, 1.0, SQRT2, SQRT2, SQRT2)
SWAP = (0, 2, 1, 3, 5, 4)
NORMAL_SCALE = (lam_ref + mu_ref) / (lam_ref + 2.0 * mu_ref)
GREEN_SCALE = 2.0 * NORMAL_SCALE
INVERSE_SCALE = -2.0 / (mu_ref * VOX) / GREEN_SCALE
AXIS_SCALE = -2.0 / PLANE / INVERSE_SCALE
OFFSET_SCALE = 2.0 / INVERSE_SCALE
AXIS_GREEN = {0: 1.0 / (lam_ref + 2.0 * mu_ref), 4: 0.5 / mu_ref, 5: 0.5 / mu_ref}
HIGHEST = lax.Precision.HIGHEST


def shape_gradients():
    lower = 0.5 - 0.5 / math.sqrt(3.0)
    upper = 0.5 + 0.5 / math.sqrt(3.0)
    table = np.zeros((8, 8, 3))
    for corner in range(8):
        bits = (corner >> 2 & 1, corner >> 1 & 1, corner & 1)
        for point in range(8):
            coords = [upper if point >> shift & 1 else lower for shift in (2, 1, 0)]
            factors = [c if b else 1.0 - c for c, b in zip(coords, bits)]
            for axis in range(3):
                entry = 1.0 if bits[axis] else -1.0
                for other in range(3):
                    if other != axis:
                        entry *= factors[other]
                table[corner, point, axis] = entry
    return table


def element_tables():
    gradient = shape_gradients()
    strain = np.zeros((6, RVES, 3, 16))
    force = np.zeros((3, 16, 6, RVES))
    for r in range(RVES):
        e, q = divmod(r, 8)
        for a in range(8):
            j = 2 * a + e
            for c, (k, h) in enumerate(component_pairs):
                strain[c, r, k, j] += 0.5 * gradient[a, q, h]
                strain[c, r, h, j] += 0.5 * gradient[a, q, k]
            for i in range(3):
                for h in range(3):
                    force[i, j, component_index[tuple(sorted((i, h)))], r] += (
                        0.125 * gradient[a, q, h]
                    )
    return strain.reshape(96, 48), force.reshape(48, 96)


def wave(m):
    return m if m < NV // 2 else m - NV


def lane_waves():
    chosen, seen = [], set()
    for ky in range(NV):
        for kz in range(NV):
            partner = (-ky % NV, -kz % NV)
            if (ky, kz) == partner or (ky, kz) in seen:
                continue
            seen.update(((ky, kz), partner))
            chosen.append((ky, kz))
    return chosen


def plane_tables():
    y, z = np.divmod(np.arange(PLANE), NV)
    forward = np.zeros((PLANE, 2 * LANES))
    for lane, (ky, kz) in enumerate(lane_waves()):
        angle = 2.0 * np.pi / NV * ((ky * y + kz * z) % NV)
        forward[:, lane] = np.cos(angle)
        forward[:, LANES + lane] = -np.sin(angle)
    forward[:, 126] = 1.0 - 2.0 * (y % 2)
    forward[:, LANES + 126] = 1.0 - 2.0 * (z % 2)
    forward[:, 127] = 1.0 - 2.0 * ((y + z) % 2)
    forward[:, LANES + 127] = 1.0
    inverse = forward.T.copy()
    inverse[[126, 127, LANES + 126, LANES + 127]] *= 0.5
    return forward, inverse * INVERSE_SCALE


def split_table(table):
    high = table.astype(ml_dtypes.bfloat16)
    low = (table - high.astype(np.float64)).astype(ml_dtypes.bfloat16)
    return np.concatenate([high, low], axis=0)


def green_tables():
    waves = lane_waves() + [(8, 0), (8, 8)]
    out = np.zeros((NV, 12, LANES))
    for kx in range(NV):
        for lane, (ky, kz) in enumerate(waves):
            index = (kx, ky, kz)
            m = np.array([wave(v) for v in index], float)
            back = np.array([wave(-v % NV) for v in index], float)
            length = np.linalg.norm(m)
            if length == 0:
                continue
            n, b = m / length, back / length
            square = n * n
            pair = lambda k, h: 0.5 * (n[k] * n[h] + b[k] * b[h])
            p = [pair(1, 2), pair(0, 2), pair(0, 1)]
            out[kx, 0:3, lane] = square
            out[kx, 3:6, lane] = [v / SQRT2 for v in p]
            for o in range(3):
                k, h = [axis for axis in range(3) if axis != o]
                out[kx, 6 + o, lane] = (
                    0.5 * (square[k] + square[h])
                    - 2.0 * NORMAL_SCALE * square[k] * square[h]
                )
                out[kx, 9 + o, lane] = p[o] * (0.5 - 2.0 * NORMAL_SCALE * square[o])
    return out * GREEN_SCALE


def twiddle(re, im, power, sign):
    power %= 16
    if power == 0:
        return re, im
    if power == 4:
        return (im, -re) if sign < 0 else (-im, re)
    angle = 2.0 * math.pi * power / 16.0
    c, s = math.cos(angle), sign * math.sin(angle)
    if power % 4 == 2:
        root = math.sqrt(0.5)
        cs, ss = math.copysign(1.0, c), math.copysign(1.0, s)
        a = re if cs > 0 else -re
        b = im if cs > 0 else -im
        if cs * ss > 0:
            real, imag = (re - im), (re + im)
        else:
            real, imag = (re + im), (im - re)
        return real * (cs * root), imag * (cs * root)
    return re * c - im * s, re * s + im * c


def dft4(v, sign):
    (ar, ai), (br, bi), (cr, ci), (dr, di) = v
    sr, si, tr, ti = ar + cr, ai + ci, ar - cr, ai - ci
    ur, ui, wr, wi = br + dr, bi + di, br - dr, bi - di
    if sign < 0:
        return [
            (sr + ur, si + ui),
            (tr + wi, ti - wr),
            (sr - ur, si - ui),
            (tr - wi, ti + wr),
        ]
    return [
        (sr + ur, si + ui),
        (tr - wi, ti + wr),
        (sr - ur, si - ui),
        (tr + wi, ti - wr),
    ]


def dft16_first(values, first, sign):
    inner = dft4(values, sign)
    return [twiddle(*inner[k], first * k, sign) for k in range(4)]


def green(t, tab):
    xyz = [tab[a] * t[a] for a in range(3)]
    d = (xyz[0] + xyz[1]) + xyz[2]
    o = [tab[3 + a] * t[3 + a] for a in range(3)]
    sums = [o[1] + o[2], o[0] + o[2], o[0] + o[1]]
    s = sums[0] + o[0]
    m = 0.5 * d + s
    out = [(xyz[a] + sums[a]) - tab[a] * m for a in range(3)]
    for a in range(3):
        k, h = [axis for axis in range(3) if axis != a]
        value = tab[3 + a] * ((t[k] + t[h]) - d) + tab[6 + a] * t[3 + a]
        value = value + (tab[9 + h] * t[3 + k] + tab[9 + k] * t[3 + h])
        out.append(value)
    return out


def split(value):
    high = value.astype(jnp.bfloat16)
    low = (value - high.astype(jnp.float32)).astype(jnp.bfloat16)
    return high, low


def product(high, low, table_ref):
    f32 = jnp.float32
    rows = high.shape[0]
    both = jnp.concatenate([low, high], axis=0)
    both = jnp.dot(both, table_ref[:PLANE], preferred_element_type=f32)
    rest = jnp.dot(high, table_ref[PLANE:], preferred_element_type=f32)
    return (both[:rows] + both[rows:]) + rest


def exact(left, right):
    return jnp.dot(left, right, precision=HIGHEST, preferred_element_type=jnp.float32)


def from_scalars(scalars, axis, shape):
    place = lax.broadcasted_iota(jnp.int32, shape, axis)
    out = jnp.full(shape, -1, jnp.int32)
    for index, value in enumerate(scalars):
        out = jnp.where(place == index, value, out)
    return out


def column(values):
    return from_scalars(values, 0, (SLOTS, LANES))


def pick(low, high, rows_of):
    place = rows_of & 7
    low = jnp.take_along_axis(low, place, axis=0, mode="promise_in_bounds")
    high = jnp.take_along_axis(high, place, axis=0, mode="promise_in_bounds")
    return jnp.where(rows_of >= SLOTS, high, low)


def prepare_kernel(
    counts_in,
    fluctuation_in,
    phases_in,
    damage_in,
    start_home,
    places_home,
    start,
    places,
    order,
    sorted_counts,
    where_is,
    counts,
    fluctuation,
    phases,
    damage,
    in_done,
    out_done,
):
    arrivals = [
        pltpu.make_async_copy(source, target, in_done.at[n])
        for n, (source, target) in enumerate(
            [(counts_in, counts), (phases_in, phases), (damage_in, damage)]
            + [(fluctuation_in.at[c], fluctuation.at[c]) for c in range(6)]
        )
    ]
    for arrival in arrivals:
        arrival.start()
    arrivals[0].wait()
    values = [counts[r] for r in range(RVES)]
    for r in range(RVES):
        rank = jnp.int32(0)
        for j in range(RVES):
            if j != r:
                ahead = values[j] >= values[r] if j < r else values[j] > values[r]
                rank = rank + ahead.astype(jnp.int32)
        place = jnp.where(rank < SLOTS, rank, RVES + SLOTS - 1 - rank)
        order[place] = r
        sorted_counts[place] = values[r]
        where_is[r] = place
    for half in range(2):
        places[half] = column([order[half * SLOTS + s] for s in range(SLOTS)])
        places[2 + half] = column([where_is[half * SLOTS + s] for s in range(SLOTS)])
    places[4] = column([sorted_counts[s] for s in range(SLOTS)])
    places[5] = column([sorted_counts[s] + sorted_counts[SLOTS + s] for s in range(SLOTS)])
    for arrival in arrivals[1:]:
        arrival.wait()

    departures = [pltpu.make_async_copy(places, places_home, out_done.at[4])]
    departures[0].start()

    def load(n, k):
        x = 4 * n + k
        for side in range(2):
            lanes = pl.ds(pl.multiple_of(x * PLANE + side * LANES, LANES), LANES)
            place = pl.ds(pl.multiple_of((k * 4 + n) * SLOTS, SLOTS), SLOTS)
            cut = slice(side * LANES, (side + 1) * LANES)
            phase = phases[:, lanes]
            soft = 1.0 - damage[:, lanes]
            soft = soft * soft + 0.05
            shear = soft * jnp.where(
                phase == 0,
                2.0 * MU_PHASE[0],
                jnp.where(phase == 1, 2.0 * MU_PHASE[1], 2.0 * MU_PHASE[2]),
            )
            second = soft * jnp.where(
                phase == 0, LAM_PHASE[0], jnp.where(phase == 1, LAM_PHASE[1], LAM_PHASE[2])
            )
            for half in range(2):
                rows_of = places[half]
                start[half, 6, place, cut] = pick(shear[:SLOTS], shear[SLOTS:], rows_of)
                start[half, 7, place, cut] = pick(second[:SLOTS], second[SLOTS:], rows_of)
                for c in range(6):
                    start[half, c, place, cut] = pick(
                        fluctuation[c, :SLOTS, lanes], fluctuation[c, SLOTS:, lanes], rows_of
                    )
        return k

    for k in range(4):
        lax.fori_loop(0, 4, load, k)
        part = pl.ds(k * 32, 32)
        departures.append(
            pltpu.make_async_copy(start.at[:, :, part], start_home.at[:, :, part], out_done.at[k])
        )
        departures[-1].start()
    for departure in departures:
        departure.wait()


def finish_kernel(
    state_in, macro_in, places_in, fluctuation_home, state, macro, places, fluctuation, in_done, out_done
):
    arrivals = [
        pltpu.make_async_copy(macro_in, macro, in_done.at[4]),
        pltpu.make_async_copy(places_in, places, in_done.at[5]),
    ]
    for k in range(4):
        part = pl.ds(k * 32, 32)
        arrivals.append(
            pltpu.make_async_copy(
                state_in.at[:, :, part], state.at[:, :, part], in_done.at[k]
            )
        )
    for arrival in arrivals:
        arrival.start()

    def departure(x):
        lanes = pl.ds(pl.multiple_of(x * PLANE, PLANE), PLANE)
        return pltpu.make_async_copy(
            fluctuation.at[:, :, lanes], fluctuation_home.at[:, :, lanes], out_done.at[x]
        )

    def gather(n, k):
        x = 4 * n + k
        place = pl.ds(pl.multiple_of((k * 4 + n) * SLOTS, SLOTS), SLOTS)
        for side in range(2):
            cut = slice(side * LANES, (side + 1) * LANES)
            lanes = pl.ds(pl.multiple_of(x * PLANE + side * LANES, LANES), LANES)
            for c in range(6):
                ends = [
                    state[1 - half, c, place, cut] * (1.0 / MANDEL[c]) - macro[half, c]
                    for half in range(2)
                ]
                for block in range(2):
                    fluctuation[c, block * SLOTS : (block + 1) * SLOTS, lanes] = pick(
                        *ends, places[2 + block]
                    )
        departure(x).start()
        return k

    def depart(x, carry):
        departure(x).wait()
        return carry

    for arrival in arrivals[:2]:
        arrival.wait()
    for k in range(4):
        arrivals[2 + k].wait()
        lax.fori_loop(0, 4, gather, k)
    lax.fori_loop(0, NV, depart, 0)


def collect_kernel(
    elem, received, external_force, residual_home, pool_home, residual_force, pool_stress, out_done
):
    total = jnp.sum(received[...].reshape(LANES, LANES), axis=0, keepdims=True)
    node = lax.broadcasted_iota(jnp.int32, (2, 3), 0)
    residual_force[...] = (
        jnp.where(node == 0, total[:, 0:3], total[:, 3:6]) - external_force[...]
    )
    own = pl.ds(pl.multiple_of(elem[0] * RVES, RVES), RVES)
    pool_stress[...] = received[own].reshape(RVES, LANES).T[6:12, :]
    departures = [
        pltpu.make_async_copy(residual_force, residual_home, out_done.at[0]),
        pltpu.make_async_copy(pool_stress, pool_home, out_done.at[1]),
    ]
    for departure in departures:
        departure.start()
    for departure in departures:
        departure.wait()


def sweep_kernel(
    elem,
    motion_in,
    routing_in,
    connectivity_in,
    places_in,
    line_tables_in,
    start_in,
    plane_tables_in,
    state,
    macro,
    sent,
    motion,
    routing,
    connectivity,
    places,
    line_tables,
    start,
    plane_tables,
    table_rows,
    rows,
    parts,
    stresses,
    plane,
    back,
    lines,
    back_lines,
    correction,
    offsets,
    means,
    in_done,
):
    f32 = jnp.float32
    arrivals = [
        pltpu.make_async_copy(source, target, in_done.at[n])
        for n, (source, target) in enumerate(
            [
                (motion_in, motion),
                (routing_in, routing),
                (connectivity_in, connectivity),
                (places_in, places),
                (line_tables_in, line_tables),
                (start_in.at[0], start.at[0]),
                (start_in.at[1], start.at[1]),
                (plane_tables_in, plane_tables),
            ]
        )
    ]
    for arrival in arrivals:
        arrival.start()
    for arrival in arrivals[:5]:
        arrival.wait()
    forward, inverse = plane_tables.at[0], plane_tables.at[1]
    nodes = [connectivity[e, a] for a in range(8) for e in range(2)]
    node_rows = from_scalars(nodes, 0, (16, LANES))
    holder = (lax.broadcasted_iota(jnp.int32, (16, LANES), 1) == (node_rows >> 1)).astype(f32)
    corner = exact(holder, motion[...].reshape(LANES, LANES))
    odd = (node_rows & 1) == 1
    moved = [
        jnp.where(
            odd,
            jnp.broadcast_to(corner[:, 3 + i : 4 + i], (16, LANES)),
            jnp.broadcast_to(corner[:, i : i + 1], (16, LANES)),
        )
        for i in range(3)
    ]
    moved = jnp.concatenate(moved + [jnp.zeros((LANES - 48, LANES), f32)], axis=0)
    for row in range(NV * 12):
        table_rows[row] = jnp.broadcast_to(line_tables[row : row + 1, :], (SLOTS, LANES))
    rows[0:96, :] = exact(line_tables[NV * 12 : NV * 12 + 96, :], moved)
    for half in range(2):
        for c in range(6):
            low = rows[c * RVES : c * RVES + SLOTS, :]
            high = rows[c * RVES + SLOTS : (c + 1) * RVES, :]
            macro[half, c] = pick(low, high, places[half])

    lane = lax.broadcasted_iota(jnp.int32, (SLOTS, LANES), 1)
    first_rows, total_rows = places[4], places[5]
    limit = jnp.max(total_rows.astype(f32)).astype(jnp.int32)

    scales = [AXIS_SCALE * AXIS_GREEN.get(c, 0.0) for c in range(6)]

    def wave_part(k):
        waves = []
        for c in range(6):
            out = dft4([(lines[c, k, first, 0], lines[c, k, first, 1]) for first in range(4)], -1)
            if k == 0:
                offset = correction[c] * OFFSET_SCALE
                if c in AXIS_GREEN:
                    offset = offset - (scales[c] / NV) * out[0][1]
                offsets[c] = offset
            waves.append(out)
        for high in range(4):
            tab = [table_rows[(k + 4 * high) * 12 + t] for t in range(12)]
            real = green([waves[c][high][0] for c in range(6)], tab)
            imag = green([waves[c][high][1] for c in range(6)], tab)
            for c in range(6):
                waves[c][high] = (real[c], imag[c])
        for c in range(6):
            for residue, (re, im) in enumerate(dft16_first(waves[c], k, 1)):
                back_lines[c, residue, k, 0] = re
                back_lines[c, residue, k, 1] = im

    def to_plane(k):
        ends = []
        for c in range(6):
            ends.append(
                dft4([(back_lines[c, k, n, 0], back_lines[c, k, n, 1]) for n in range(4)], 1)
            )
        for c in range(6):
            for pair in range(2):
                re, im = [], []
                for n in (2 * pair, 2 * pair + 1):
                    own = ends[c][n][1]
                    if SWAP[c] != c:
                        own = jnp.where(lane == 126, ends[SWAP[c]][n][1], own)
                    axis_value = offsets[c]
                    if c in AXIS_GREEN:
                        row = (c * 4 + n) * SLOTS
                        axis_value = (
                            axis_value + scales[c] * plane[k, row : row + SLOTS, LANES:]
                        )
                    im.append(jnp.where(lane == 127, axis_value, own))
                    re.append(ends[c][n][0])
                value = jnp.concatenate(
                    [jnp.concatenate(re, axis=0), jnp.concatenate(im, axis=0)], axis=1
                )
                high, low = split(value)
                put = slice((c * 2 + pair) * 16, (c * 2 + pair + 1) * 16)
                parts[k, 0, put, :] = high
                parts[k, 1, put, :] = low

    def to_voxels(k):
        back[k] = product(parts[k, 0], parts[k, 1], inverse)

    def update(k, step, masks, sums):
        switch, later, active = masks
        for pair in range(2):
            place = slice((k * 2 + pair) * 16, (k * 2 + pair + 1) * 16)
            strain = []
            for c in range(6):
                if step is None:
                    for half in (1, 0):
                        own = jnp.concatenate([macro[half, c]] * 2, axis=0)
                        own = jnp.concatenate([own, own], axis=1)
                        ended = (start[half, c, place, :] + own) * MANDEL[c]
                        state[half, c, place, :] = ended
                else:
                    ended = state[0, c, place, :]
                    put = slice((c * 2 + pair) * 16, (c * 2 + pair + 1) * 16)
                    ended = ended + back[k, put, :]
                    waiting = state[1, c, place, :]
                    pltpu.store(state.at[1, c, place, :], ended, mask=switch)
                    ended = jnp.where(switch, waiting, ended)
                    state[0, c, place, :] = ended
                strain.append(ended)
            shear, pressure = start[0, 6, place, :], start[0, 7, place, :]
            if step is not None:
                shear = active * jnp.where(later, start[1, 6, place, :], shear)
                pressure = active * jnp.where(later, start[1, 7, place, :], pressure)
            pressure = pressure * ((strain[0] + strain[1]) + strain[2])
            for c in range(6):
                stress = shear * strain[c]
                if c < 3:
                    stress = stress + pressure
                high, low = split(stress)
                put = slice((c * 2 + pair) * 16, (c * 2 + pair + 1) * 16)
                stresses[k, 0, put, :] = high
                stresses[k, 1, put, :] = low
                own = strain[c][:SLOTS] + strain[c][SLOTS:]
                sums[c] = own if sums[c] is None else sums[c] + own

    def to_waves(k):
        plane[k] = product(stresses[k, 0], stresses[k, 1], forward)

    def from_plane(k):
        for c in range(6):
            line = []
            for n in range(4):
                row = (c * 4 + n) * SLOTS
                re = plane[k, row : row + SLOTS, :LANES]
                im = plane[k, row : row + SLOTS, LANES:]
                if SWAP[c] != c:
                    row = (SWAP[c] * 4 + n) * SLOTS
                    im = jnp.where(lane == 126, plane[k, row : row + SLOTS, LANES:], im)
                line.append((re, im))
            for residue, (re, im) in enumerate(dft16_first(line, k, -1)):
                lines[c, residue, k, 0] = re
                lines[c, residue, k, 1] = im

    def correct(later, active, sums):
        for c in range(6):
            mean = jnp.sum(sums[c], axis=1, keepdims=True) * (1.0 / VOX)
            own = macro[0, c] if later is None else jnp.where(later, macro[1, c], macro[0, c])
            own = own * MANDEL[c] - mean
            correction[c] = own if active is None else own * active

    def wide(mask):
        mask = jnp.concatenate([mask, mask], axis=1)
        return jnp.concatenate([mask, mask], axis=0)

    def sweep(step, carry):
        step = step + 1
        switch, later = first_rows == step, first_rows <= step
        active = (step < total_rows).astype(f32)
        masks = (wide(switch), wide(later), wide(active))
        sums = [None] * 6
        for k in range(4):
            wave_part(k)
        stages = [
            to_plane,
            to_voxels,
            lambda k: update(k, step, masks, sums),
            to_waves,
            from_plane,
        ]
        for stage in stages:
            for k in range(4):
                stage(k)
        correct(later, active, sums)
        return carry

    for arrival in arrivals[5:]:
        arrival.wait()
    sums = [None] * 6
    for k in range(4):
        update(k, None, (None, None, None), sums)
        to_waves(k)
    for k in range(4):
        from_plane(k)
    correct(None, None, sums)
    lax.fori_loop(0, limit, sweep, 0)

    def gather(x, sums):
        place = pl.ds(pl.multiple_of(x * 2 * SLOTS, 2 * SLOTS), 2 * SLOTS)
        out = []
        for half in range(2):
            strain = [state[1 - half, c, place, :] for c in range(6)]
            shear = start[half, 6, place, :]
            pressure = start[half, 7, place, :] * ((strain[0] + strain[1]) + strain[2])
            for c in range(6):
                stress = shear * strain[c]
                if c < 3:
                    stress = stress + pressure
                stress = stress[:SLOTS] + stress[SLOTS:]
                out.append(sums[6 * half + c] + (stress[:, :LANES] + stress[:, LANES:]))
        return tuple(out)

    sums = lax.fori_loop(
        0, NV // 2, gather, tuple(jnp.zeros((SLOTS, LANES), f32) for _ in range(12))
    )
    for half in range(2):
        for c in range(6):
            mean = jnp.sum(sums[6 * half + c], axis=1, keepdims=True)
            mean = mean * (1.0 / (VOX * MANDEL[c]))
            means[half, c] = jnp.broadcast_to(mean, (SLOTS, LANES))
    for block in range(2):
        for c in range(6):
            base = c * RVES + block * SLOTS
            rows[base : base + SLOTS, :] = pick(means[0, c], means[1, c], places[2 + block])

    stress_rows = jnp.concatenate([rows[0:96, :], jnp.zeros((32, LANES), f32)], axis=0)
    force = exact(line_tables[NV * 12 + 96 :, :], stress_rows)
    lane_of = lax.broadcasted_iota(jnp.int32, (16, LANES), 1)
    right = []
    for low in range(2):
        block = jnp.zeros((16, LANES), f32)
        for i in range(3):
            block = jnp.where(lane_of == 3 * low + i, force[16 * i : 16 * i + 16], block)
        right.append(block)
    block = jnp.zeros((16, LANES), f32)
    for c in range(6):
        block = jnp.where(lane_of == 6 + c, rows[c * RVES : (c + 1) * RVES, :], block)
    right.append(block)
    right.append(jnp.zeros((80, LANES), f32))
    target = [jnp.where((n & 1) == 0, n >> 1, -1) for n in nodes]
    target += [jnp.where((n & 1) == 1, n >> 1, -1) for n in nodes]
    target += [elem[0] * RVES + routing[r] for r in range(RVES)]
    wanted = from_scalars(target, 1, (LANES, LANES))
    taken = (lax.broadcasted_iota(jnp.int32, (LANES, LANES), 0) == wanted).astype(f32)
    sent[...] = exact(taken, jnp.concatenate(right, axis=0)).reshape(LANES, 1, LANES)


def tables():
    plane_table = np.stack([split_table(table) for table in plane_tables()])
    strain_table, force_table = element_tables()
    line_table = np.zeros((NV * 12 + 96 + 48, LANES), np.float32)
    line_table[: NV * 12] = green_tables().reshape(NV * 12, LANES)
    line_table[NV * 12 : NV * 12 + 96, :48] = strain_table
    line_table[NV * 12 + 96 :, :96] = force_table
    return plane_table, line_table


SMEM = pl.BlockSpec(memory_space=pltpu.SMEM)
VMEM = pl.BlockSpec(memory_space=pltpu.VMEM)
HBM = pl.BlockSpec(memory_space=pltpu.HBM)
VMEM_MIB = 40
SOLVE_MIB = 54
PREPARE_MIB = 61
FINISH_MIB = 61
PARAMS = pltpu.CompilerParams(vmem_limit_bytes=VMEM_MIB * 1024 * 1024)


def of(shape, kind=jnp.float32):
    return jax.ShapeDtypeStruct(shape, kind)


def prepare(counts, fluctuation, phases, damage):
    f32 = jnp.float32
    return pl.pallas_call(
        prepare_kernel,
        out_shape=(
            of((2, 8, ROWS, PLANE)),
            of((6, SLOTS, LANES), jnp.int32),
        ),
        in_specs=[HBM] * 4,
        out_specs=(HBM, HBM),
        scratch_shapes=[
            pltpu.VMEM((2, 8, ROWS, PLANE), f32),
            pltpu.VMEM((6, SLOTS, LANES), jnp.int32),
            pltpu.SMEM((RVES,), jnp.int32),
            pltpu.SMEM((RVES,), jnp.int32),
            pltpu.SMEM((RVES,), jnp.int32),
            pltpu.SMEM((RVES,), jnp.int32),
            pltpu.VMEM((6, RVES, VOX), f32),
            pltpu.VMEM((RVES, VOX), jnp.int32),
            pltpu.VMEM((RVES, VOX), f32),
            pltpu.SemaphoreType.DMA((9,)),
            pltpu.SemaphoreType.DMA((5,)),
        ],
        cost_estimate=pl.CostEstimate(
            flops=8_000_000, bytes_accessed=8_000_000, transcendentals=0
        ),
        compiler_params=pltpu.CompilerParams(vmem_limit_bytes=PREPARE_MIB * 1024 * 1024),
        name="prepare_rves",
    )(counts, fluctuation, phases, damage)


def solve(routing, connectivity, elem, motion, prepared):
    f32 = jnp.float32
    plane_table, line_table = tables()
    return pl.pallas_call(
        sweep_kernel,
        out_shape=(of((2, 6, ROWS, PLANE)), of((2, 6, SLOTS, LANES)), of((LANES, 1, LANES))),
        in_specs=[SMEM] + [HBM] * 7,
        out_specs=(VMEM,) * 3,
        scratch_shapes=[
            pltpu.VMEM((LANES, 1, LANES), f32),
            pltpu.SMEM((RVES,), jnp.int32),
            pltpu.SMEM((2, 8), jnp.int32),
            pltpu.VMEM((6, SLOTS, LANES), jnp.int32),
            pltpu.VMEM(line_table.shape, f32),
            pltpu.VMEM((2, 8, ROWS, PLANE), f32),
            pltpu.VMEM(plane_table.shape, jnp.bfloat16),
            pltpu.VMEM((NV * 12, SLOTS, LANES), f32),
            pltpu.VMEM((96, LANES), f32),
            pltpu.VMEM((4, 2, 192, PLANE), jnp.bfloat16),
            pltpu.VMEM((4, 2, 192, PLANE), jnp.bfloat16),
            pltpu.VMEM((4, 192, PLANE), f32),
            pltpu.VMEM((4, 192, PLANE), f32),
            pltpu.VMEM((6, 4, 4, 2, SLOTS, LANES), f32),
            pltpu.VMEM((6, 4, 4, 2, SLOTS, LANES), f32),
            pltpu.VMEM((6, SLOTS, LANES), f32),
            pltpu.VMEM((6, SLOTS, LANES), f32),
            pltpu.VMEM((2, 6, SLOTS, LANES), f32),
            pltpu.SemaphoreType.DMA((8,)),
        ],
        compiler_params=pltpu.CompilerParams(vmem_limit_bytes=SOLVE_MIB * 1024 * 1024),
        name="solve_rves",
    )(
        elem,
        motion,
        routing,
        connectivity,
        prepared[1],
        jnp.asarray(line_table),
        prepared[0],
        jnp.asarray(plane_table),
    )


def finish(state, macro, places):
    return pl.pallas_call(
        finish_kernel,
        out_shape=of((6, RVES, VOX)),
        in_specs=[HBM] * 3,
        out_specs=HBM,
        scratch_shapes=[
            pltpu.VMEM((2, 6, ROWS, PLANE), jnp.float32),
            pltpu.VMEM((2, 6, SLOTS, LANES), jnp.float32),
            pltpu.VMEM((6, SLOTS, LANES), jnp.int32),
            pltpu.VMEM((6, RVES, VOX), jnp.float32),
            pltpu.SemaphoreType.DMA((6,)),
            pltpu.SemaphoreType.DMA((NV,)),
        ],
        cost_estimate=pl.CostEstimate(
            flops=4_000_000, bytes_accessed=4_000_000, transcendentals=0
        ),
        compiler_params=pltpu.CompilerParams(vmem_limit_bytes=FINISH_MIB * 1024 * 1024),
        name="finish_rves",
    )(state, macro, places)


def exchange(rows):
    return lax.all_to_all(rows, ("elem", "rve"), split_axis=0, concat_axis=0, tiled=True)


def shards(
    displacement,
    connectivity,
    fluctuation,
    phases,
    damage,
    iteration_counts,
    routing,
    external_force,
):
    own = jnp.pad(displacement.T.reshape(1, 1, 6), ((0, 0), (0, 0), (0, LANES - 6)))
    own = jnp.broadcast_to(own, (LANES, 1, LANES))
    motion = exchange(own)
    elem = lax.axis_index("elem").astype(jnp.int32).reshape(1)
    prepared = prepare(
        iteration_counts, jnp.transpose(fluctuation, (1, 0, 2)), phases, damage
    )
    state, macro, sent = solve(routing, connectivity.T, elem, motion, prepared)
    received = exchange(sent)
    fluctuation_out = jnp.transpose(finish(state, macro, prepared[1]), (1, 0, 2))
    residual_force, pool_stress = pl.pallas_call(
        collect_kernel,
        out_shape=(of((2, 3)), of((6, RVES))),
        in_specs=[SMEM, VMEM, VMEM],
        out_specs=(HBM, HBM),
        scratch_shapes=[
            pltpu.VMEM((2, 3), jnp.float32),
            pltpu.VMEM((6, RVES), jnp.float32),
            pltpu.SemaphoreType.DMA((2,)),
        ],
        compiler_params=PARAMS,
        name="collect_results",
    )(elem, received, external_force.T)
    return (residual_force.T, fluctuation_out, pool_stress.T)


def solution(mesh):
    both = ("elem", "rve")
    return jax.shard_map(
        shards,
        mesh=mesh,
        in_specs=(
            P(None, both),
            P(None, both),
            P(both, None, None),
            P(both, None),
            P(both, None),
            P(both),
            P(both),
            P(None, both),
        ),
        out_specs=(P(None, both), P(both, None, None), P(both, None)),
        check_vma=False,
    )
```

```python
import math

import jax
import jax.numpy as jnp
import ml_dtypes
import numpy as np
from jax import lax
from jax.experimental import pallas as pl
from jax.experimental.pallas import tpu as pltpu
from jax.sharding import PartitionSpec as P

NV = 16
PLANE = NV * NV
VOX = NV**3
LANES = 128
SLOTS = 8
RVES = 16
ROWS = NV * SLOTS
MU_PHASE = (0.1, 0.4, 2.0)
LAM_PHASE = (0.15, 0.6, 1.0)
mu_ref = 1.053
lam_ref = 0.5295
component_pairs = ((0, 0), (1, 1), (2, 2), (1, 2), (0, 2), (0, 1))
component_index = {tuple(sorted(pair)): c for c, pair in enumerate(component_pairs)}
SQRT2 = math.sqrt(2.0)
MANDEL = (1.0, 1.0, 1.0, SQRT2, SQRT2, SQRT2)
SWAP = (0, 2, 1, 3, 5, 4)
NORMAL_SCALE = (lam_ref + mu_ref) / (lam_ref + 2.0 * mu_ref)
GREEN_SCALE = 2.0 * NORMAL_SCALE
INVERSE_SCALE = -2.0 / (mu_ref * VOX) / GREEN_SCALE
AXIS_SCALE = -2.0 / PLANE / INVERSE_SCALE
OFFSET_SCALE = 2.0 / INVERSE_SCALE
AXIS_GREEN = {0: 1.0 / (lam_ref + 2.0 * mu_ref), 4: 0.5 / mu_ref, 5: 0.5 / mu_ref}
HIGHEST = lax.Precision.HIGHEST


def shape_gradients():
    lower = 0.5 - 0.5 / math.sqrt(3.0)
    upper = 0.5 + 0.5 / math.sqrt(3.0)
    table = np.zeros((8, 8, 3))
    for corner in range(8):
        bits = (corner >> 2 & 1, corner >> 1 & 1, corner & 1)
        for point in range(8):
            coords = [upper if point >> shift & 1 else lower for shift in (2, 1, 0)]
            factors = [c if b else 1.0 - c for c, b in zip(coords, bits)]
            for axis in range(3):
                entry = 1.0 if bits[axis] else -1.0
                for other in range(3):
                    if other != axis:
                        entry *= factors[other]
                table[corner, point, axis] = entry
    return table


def element_tables():
    gradient = shape_gradients()
    strain = np.zeros((6, RVES, 3, 16))
    force = np.zeros((3, 16, 6, RVES))
    for r in range(RVES):
        e, q = divmod(r, 8)
        for a in range(8):
            j = 2 * a + e
            for c, (k, h) in enumerate(component_pairs):
                strain[c, r, k, j] += 0.5 * gradient[a, q, h]
                strain[c, r, h, j] += 0.5 * gradient[a, q, k]
            for i in range(3):
                for h in range(3):
                    force[i, j, component_index[tuple(sorted((i, h)))], r] += (
                        0.125 * gradient[a, q, h]
                    )
    return strain.reshape(96, 48), force.reshape(48, 96)


def wave(m):
    return m if m < NV // 2 else m - NV


def lane_waves():
    chosen, seen = [], set()
    for ky in range(NV):
        for kz in range(NV):
            partner = (-ky % NV, -kz % NV)
            if (ky, kz) == partner or (ky, kz) in seen:
                continue
            seen.update(((ky, kz), partner))
            chosen.append((ky, kz))
    return chosen


def plane_tables():
    y, z = np.divmod(np.arange(PLANE), NV)
    forward = np.zeros((PLANE, 2 * LANES))
    for lane, (ky, kz) in enumerate(lane_waves()):
        angle = 2.0 * np.pi / NV * ((ky * y + kz * z) % NV)
        forward[:, lane] = np.cos(angle)
        forward[:, LANES + lane] = -np.sin(angle)
    forward[:, 126] = 1.0 - 2.0 * (y % 2)
    forward[:, LANES + 126] = 1.0 - 2.0 * (z % 2)
    forward[:, 127] = 1.0 - 2.0 * ((y + z) % 2)
    forward[:, LANES + 127] = 1.0
    inverse = forward.T.copy()
    inverse[[126, 127, LANES + 126, LANES + 127]] *= 0.5
    return forward, inverse * INVERSE_SCALE


def split_table(table):
    high = table.astype(ml_dtypes.bfloat16)
    low = (table - high.astype(np.float64)).astype(ml_dtypes.bfloat16)
    return np.concatenate([high, low], axis=0)


def green_tables():
    waves = lane_waves() + [(8, 0), (8, 8)]
    out = np.zeros((NV, 12, LANES))
    for kx in range(NV):
        for lane, (ky, kz) in enumerate(waves):
            index = (kx, ky, kz)
            m = np.array([wave(v) for v in index], float)
            back = np.array([wave(-v % NV) for v in index], float)
            length = np.linalg.norm(m)
            if length == 0:
                continue
            n, b = m / length, back / length
            square = n * n
            pair = lambda k, h: 0.5 * (n[k] * n[h] + b[k] * b[h])
            p = [pair(1, 2), pair(0, 2), pair(0, 1)]
            out[kx, 0:3, lane] = square
            out[kx, 3:6, lane] = [v / SQRT2 for v in p]
            for o in range(3):
                k, h = [axis for axis in range(3) if axis != o]
                out[kx, 6 + o, lane] = (
                    0.5 * (square[k] + square[h])
                    - 2.0 * NORMAL_SCALE * square[k] * square[h]
                )
                out[kx, 9 + o, lane] = p[o] * (0.5 - 2.0 * NORMAL_SCALE * square[o])
    return out * GREEN_SCALE


def twiddle(re, im, power, sign):
    power %= 16
    if power == 0:
        return re, im
    if power == 4:
        return (im, -re) if sign < 0 else (-im, re)
    angle = 2.0 * math.pi * power / 16.0
    c, s = math.cos(angle), sign * math.sin(angle)
    if power % 4 == 2:
        root = math.sqrt(0.5)
        cs, ss = math.copysign(1.0, c), math.copysign(1.0, s)
        a = re if cs > 0 else -re
        b = im if cs > 0 else -im
        if cs * ss > 0:
            real, imag = (re - im), (re + im)
        else:
            real, imag = (re + im), (im - re)
        return real * (cs * root), imag * (cs * root)
    return re * c - im * s, re * s + im * c


def dft4(v, sign):
    (ar, ai), (br, bi), (cr, ci), (dr, di) = v
    sr, si, tr, ti = ar + cr, ai + ci, ar - cr, ai - ci
    ur, ui, wr, wi = br + dr, bi + di, br - dr, bi - di
    if sign < 0:
        return [
            (sr + ur, si + ui),
            (tr + wi, ti - wr),
            (sr - ur, si - ui),
            (tr - wi, ti + wr),
        ]
    return [
        (sr + ur, si + ui),
        (tr - wi, ti + wr),
        (sr - ur, si - ui),
        (tr + wi, ti - wr),
    ]


def dft16_first(values, first, sign):
    inner = dft4(values, sign)
    return [twiddle(*inner[k], first * k, sign) for k in range(4)]


def green(t, tab):
    xyz = [tab[a] * t[a] for a in range(3)]
    d = (xyz[0] + xyz[1]) + xyz[2]
    o = [tab[3 + a] * t[3 + a] for a in range(3)]
    sums = [o[1] + o[2], o[0] + o[2], o[0] + o[1]]
    s = sums[0] + o[0]
    m = 0.5 * d + s
    out = [(xyz[a] + sums[a]) - tab[a] * m for a in range(3)]
    for a in range(3):
        k, h = [axis for axis in range(3) if axis != a]
        value = tab[3 + a] * ((t[k] + t[h]) - d) + tab[6 + a] * t[3 + a]
        value = value + (tab[9 + h] * t[3 + k] + tab[9 + k] * t[3 + h])
        out.append(value)
    return out


def split(value):
    high = value.astype(jnp.bfloat16)
    low = (value - high.astype(jnp.float32)).astype(jnp.bfloat16)
    return high, low


def product(high, low, table_ref):
    f32 = jnp.float32
    rows = high.shape[0]
    both = jnp.concatenate([low, high], axis=0)
    both = jnp.dot(both, table_ref[:PLANE], preferred_element_type=f32)
    rest = jnp.dot(high, table_ref[PLANE:], preferred_element_type=f32)
    return (both[:rows] + both[rows:]) + rest


def exact(left, right):
    return jnp.dot(left, right, precision=HIGHEST, preferred_element_type=jnp.float32)


def from_scalars(scalars, axis, shape):
    place = lax.broadcasted_iota(jnp.int32, shape, axis)
    out = jnp.full(shape, -1, jnp.int32)
    for index, value in enumerate(scalars):
        out = jnp.where(place == index, value, out)
    return out


def column(values):
    return from_scalars(values, 0, (SLOTS, LANES))


def pick(low, high, rows_of):
    place = rows_of & 7
    low = jnp.take_along_axis(low, place, axis=0, mode="promise_in_bounds")
    high = jnp.take_along_axis(high, place, axis=0, mode="promise_in_bounds")
    return jnp.where(rows_of >= SLOTS, high, low)


def prepare_kernel(
    counts_in,
    fluctuation_in,
    phases_in,
    damage_in,
    start_home,
    places_home,
    start,
    places,
    order,
    sorted_counts,
    where_is,
    counts,
    fluctuation,
    phases,
    damage,
    in_done,
    out_done,
):
    arrivals = [
        pltpu.make_async_copy(source, target, in_done.at[n])
        for n, (source, target) in enumerate(
            [(counts_in, counts), (phases_in, phases), (damage_in, damage)]
            + [(fluctuation_in.at[c], fluctuation.at[c]) for c in range(6)]
        )
    ]
    for arrival in arrivals:
        arrival.start()
    arrivals[0].wait()
    values = [counts[r] for r in range(RVES)]
    for r in range(RVES):
        rank = jnp.int32(0)
        for j in range(RVES):
            if j != r:
                ahead = values[j] >= values[r] if j < r else values[j] > values[r]
                rank = rank + ahead.astype(jnp.int32)
        place = jnp.where(rank < SLOTS, rank, RVES + SLOTS - 1 - rank)
        order[place] = r
        sorted_counts[place] = values[r]
        where_is[r] = place
    for half in range(2):
        places[half] = column([order[half * SLOTS + s] for s in range(SLOTS)])
        places[2 + half] = column([where_is[half * SLOTS + s] for s in range(SLOTS)])
    places[4] = column([sorted_counts[s] for s in range(SLOTS)])
    places[5] = column([sorted_counts[s] + sorted_counts[SLOTS + s] for s in range(SLOTS)])
    for arrival in arrivals[1:]:
        arrival.wait()

    departures = [pltpu.make_async_copy(places, places_home, out_done.at[4])]
    departures[0].start()

    def load(n, k):
        x = 4 * n + k
        for side in range(2):
            lanes = pl.ds(pl.multiple_of(x * PLANE + side * LANES, LANES), LANES)
            place = pl.ds(pl.multiple_of((k * 4 + n) * SLOTS, SLOTS), SLOTS)
            cut = slice(side * LANES, (side + 1) * LANES)
            phase = phases[:, lanes]
            soft = 1.0 - damage[:, lanes]
            soft = soft * soft + 0.05
            shear = soft * jnp.where(
                phase == 0,
                2.0 * MU_PHASE[0],
                jnp.where(phase == 1, 2.0 * MU_PHASE[1], 2.0 * MU_PHASE[2]),
            )
            second = soft * jnp.where(
                phase == 0, LAM_PHASE[0], jnp.where(phase == 1, LAM_PHASE[1], LAM_PHASE[2])
            )
            for half in range(2):
                rows_of = places[half]
                start[half, 6, place, cut] = pick(shear[:SLOTS], shear[SLOTS:], rows_of)
                start[half, 7, place, cut] = pick(second[:SLOTS], second[SLOTS:], rows_of)
                for c in range(6):
                    start[half, c, place, cut] = pick(
                        fluctuation[c, :SLOTS, lanes], fluctuation[c, SLOTS:, lanes], rows_of
                    )
        return k

    for k in range(4):
        lax.fori_loop(0, 4, load, k)
        part = pl.ds(k * 32, 32)
        departures.append(
            pltpu.make_async_copy(start.at[:, :, part], start_home.at[:, :, part], out_done.at[k])
        )
        departures[-1].start()
    for departure in departures:
        departure.wait()


def finish_kernel(
    state_in, macro_in, places_in, fluctuation_home, state, macro, places, fluctuation, in_done, out_done
):
    arrivals = [
        pltpu.make_async_copy(macro_in, macro, in_done.at[4]),
        pltpu.make_async_copy(places_in, places, in_done.at[5]),
    ]
    for k in range(4):
        part = pl.ds(k * 32, 32)
        arrivals.append(
            pltpu.make_async_copy(
                state_in.at[:, :, part], state.at[:, :, part], in_done.at[k]
            )
        )
    for arrival in arrivals:
        arrival.start()

    def departure(x):
        lanes = pl.ds(pl.multiple_of(x * PLANE, PLANE), PLANE)
        return pltpu.make_async_copy(
            fluctuation.at[:, :, lanes], fluctuation_home.at[:, :, lanes], out_done.at[x]
        )

    def gather(n, k):
        x = 4 * n + k
        place = pl.ds(pl.multiple_of((k * 4 + n) * SLOTS, SLOTS), SLOTS)
        for side in range(2):
            cut = slice(side * LANES, (side + 1) * LANES)
            lanes = pl.ds(pl.multiple_of(x * PLANE + side * LANES, LANES), LANES)
            for c in range(6):
                ends = [
                    state[1 - half, c, place, cut] * (1.0 / MANDEL[c]) - macro[half, c]
                    for half in range(2)
                ]
                for block in range(2):
                    fluctuation[c, block * SLOTS : (block + 1) * SLOTS, lanes] = pick(
                        *ends, places[2 + block]
                    )
        departure(x).start()
        return k

    def depart(x, carry):
        departure(x).wait()
        return carry

    for arrival in arrivals[:2]:
        arrival.wait()
    for k in range(4):
        arrivals[2 + k].wait()
        lax.fori_loop(0, 4, gather, k)
    lax.fori_loop(0, NV, depart, 0)


def collect_kernel(
    elem, received, external_force, residual_home, pool_home, residual_force, pool_stress, out_done
):
    total = jnp.sum(received[...].reshape(LANES, LANES), axis=0, keepdims=True)
    node = lax.broadcasted_iota(jnp.int32, (2, 3), 0)
    residual_force[...] = (
        jnp.where(node == 0, total[:, 0:3], total[:, 3:6]) - external_force[...]
    )
    own = pl.ds(pl.multiple_of(elem[0] * RVES, RVES), RVES)
    pool_stress[...] = received[own].reshape(RVES, LANES).T[6:12, :]
    departures = [
        pltpu.make_async_copy(residual_force, residual_home, out_done.at[0]),
        pltpu.make_async_copy(pool_stress, pool_home, out_done.at[1]),
    ]
    for departure in departures:
        departure.start()
    for departure in departures:
        departure.wait()


def sweep_kernel(
    elem,
    motion_in,
    routing_in,
    connectivity_in,
    places_in,
    line_tables_in,
    start_in,
    plane_tables_in,
    state,
    macro,
    sent,
    motion,
    routing,
    connectivity,
    places,
    line_tables,
    start,
    plane_tables,
    table_rows,
    rows,
    parts,
    stresses,
    plane,
    back,
    lines,
    back_lines,
    correction,
    offsets,
    means,
    in_done,
):
    f32 = jnp.float32
    arrivals = [
        pltpu.make_async_copy(source, target, in_done.at[n])
        for n, (source, target) in enumerate(
            [
                (motion_in, motion),
                (routing_in, routing),
                (connectivity_in, connectivity),
                (places_in, places),
                (line_tables_in, line_tables),
                (start_in.at[0], start.at[0]),
                (start_in.at[1], start.at[1]),
                (plane_tables_in, plane_tables),
            ]
        )
    ]
    for arrival in arrivals:
        arrival.start()
    for arrival in arrivals[:5]:
        arrival.wait()
    forward, inverse = plane_tables.at[0], plane_tables.at[1]
    nodes = [connectivity[e, a] for a in range(8) for e in range(2)]
    node_rows = from_scalars(nodes, 0, (16, LANES))
    holder = (lax.broadcasted_iota(jnp.int32, (16, LANES), 1) == (node_rows >> 1)).astype(f32)
    corner = exact(holder, motion[...].reshape(LANES, LANES))
    odd = (node_rows & 1) == 1
    moved = [
        jnp.where(
            odd,
            jnp.broadcast_to(corner[:, 3 + i : 4 + i], (16, LANES)),
            jnp.broadcast_to(corner[:, i : i + 1], (16, LANES)),
        )
        for i in range(3)
    ]
    moved = jnp.concatenate(moved + [jnp.zeros((LANES - 48, LANES), f32)], axis=0)
    for row in range(NV * 12):
        table_rows[row] = jnp.broadcast_to(line_tables[row : row + 1, :], (SLOTS, LANES))
    rows[0:96, :] = exact(line_tables[NV * 12 : NV * 12 + 96, :], moved)
    for half in range(2):
        for c in range(6):
            low = rows[c * RVES : c * RVES + SLOTS, :]
            high = rows[c * RVES + SLOTS : (c + 1) * RVES, :]
            macro[half, c] = pick(low, high, places[half])

    lane = lax.broadcasted_iota(jnp.int32, (SLOTS, LANES), 1)
    first_rows, total_rows = places[4], places[5]
    limit = jnp.max(total_rows.astype(f32)).astype(jnp.int32)

    scales = [AXIS_SCALE * AXIS_GREEN.get(c, 0.0) for c in range(6)]

    def wave_part(k):
        waves = []
        for c in range(6):
            out = dft4([(lines[c, k, first, 0], lines[c, k, first, 1]) for first in range(4)], -1)
            if k == 0:
                offset = correction[c] * OFFSET_SCALE
                if c in AXIS_GREEN:
                    offset = offset - (scales[c] / NV) * out[0][1]
                offsets[c] = offset
            waves.append(out)
        for high in range(4):
            tab = [table_rows[(k + 4 * high) * 12 + t] for t in range(12)]
            real = green([waves[c][high][0] for c in range(6)], tab)
            imag = green([waves[c][high][1] for c in range(6)], tab)
            for c in range(6):
                waves[c][high] = (real[c], imag[c])
        for c in range(6):
            for residue, (re, im) in enumerate(dft16_first(waves[c], k, 1)):
                back_lines[c, residue, k, 0] = re
                back_lines[c, residue, k, 1] = im

    def to_plane(k):
        ends = []
        for c in range(6):
            ends.append(
                dft4([(back_lines[c, k, n, 0], back_lines[c, k, n, 1]) for n in range(4)], 1)
            )
        for c in range(6):
            for pair in range(2):
                re, im = [], []
                for n in (2 * pair, 2 * pair + 1):
                    own = ends[c][n][1]
                    if SWAP[c] != c:
                        own = jnp.where(lane == 126, ends[SWAP[c]][n][1], own)
                    axis_value = offsets[c]
                    if c in AXIS_GREEN:
                        row = (c * 4 + n) * SLOTS
                        axis_value = (
                            axis_value + scales[c] * plane[k, row : row + SLOTS, LANES:]
                        )
                    im.append(jnp.where(lane == 127, axis_value, own))
                    re.append(ends[c][n][0])
                value = jnp.concatenate(
                    [jnp.concatenate(re, axis=0), jnp.concatenate(im, axis=0)], axis=1
                )
                high, low = split(value)
                put = slice((c * 2 + pair) * 16, (c * 2 + pair + 1) * 16)
                parts[k, 0, put, :] = high
                parts[k, 1, put, :] = low

    def to_voxels(k):
        back[k] = product(parts[k, 0], parts[k, 1], inverse)

    def update(k, step, masks, sums):
        switch, later, active = masks
        for pair in range(2):
            place = slice((k * 2 + pair) * 16, (k * 2 + pair + 1) * 16)
            strain = []
            for c in range(6):
                if step is None:
                    for half in (1, 0):
                        own = jnp.concatenate([macro[half, c]] * 2, axis=0)
                        own = jnp.concatenate([own, own], axis=1)
                        ended = (start[half, c, place, :] + own) * MANDEL[c]
                        state[half, c, place, :] = ended
                else:
                    ended = state[0, c, place, :]
                    put = slice((c * 2 + pair) * 16, (c * 2 + pair + 1) * 16)
                    ended = ended + back[k, put, :]
                    waiting = state[1, c, place, :]
                    pltpu.store(state.at[1, c, place, :], ended, mask=switch)
                    ended = jnp.where(switch, waiting, ended)
                    state[0, c, place, :] = ended
                strain.append(ended)
            shear, pressure = start[0, 6, place, :], start[0, 7, place, :]
            if step is not None:
                shear = active * jnp.where(later, start[1, 6, place, :], shear)
                pressure = active * jnp.where(later, start[1, 7, place, :], pressure)
            pressure = pressure * ((strain[0] + strain[1]) + strain[2])
            for c in range(6):
                stress = shear * strain[c]
                if c < 3:
                    stress = stress + pressure
                high, low = split(stress)
                put = slice((c * 2 + pair) * 16, (c * 2 + pair + 1) * 16)
                stresses[k, 0, put, :] = high
                stresses[k, 1, put, :] = low
                own = strain[c][:SLOTS] + strain[c][SLOTS:]
                sums[c] = own if sums[c] is None else sums[c] + own

    def to_waves(k):
        plane[k] = product(stresses[k, 0], stresses[k, 1], forward)

    def from_plane(k):
        for c in range(6):
            line = []
            for n in range(4):
                row = (c * 4 + n) * SLOTS
                re = plane[k, row : row + SLOTS, :LANES]
                im = plane[k, row : row + SLOTS, LANES:]
                if SWAP[c] != c:
                    row = (SWAP[c] * 4 + n) * SLOTS
                    im = jnp.where(lane == 126, plane[k, row : row + SLOTS, LANES:], im)
                line.append((re, im))
            for residue, (re, im) in enumerate(dft16_first(line, k, -1)):
                lines[c, residue, k, 0] = re
                lines[c, residue, k, 1] = im

    def correct(later, active, sums):
        for c in range(6):
            mean = jnp.sum(sums[c], axis=1, keepdims=True) * (1.0 / VOX)
            own = macro[0, c] if later is None else jnp.where(later, macro[1, c], macro[0, c])
            own = own * MANDEL[c] - mean
            correction[c] = own if active is None else own * active

    def wide(mask):
        mask = jnp.concatenate([mask, mask], axis=1)
        return jnp.concatenate([mask, mask], axis=0)

    def sweep(step, carry):
        step = step + 1
        switch, later = first_rows == step, first_rows <= step
        active = (step < total_rows).astype(f32)
        masks = (wide(switch), wide(later), wide(active))
        sums = [None] * 6
        for k in range(4):
            wave_part(k)
        stages = [
            to_plane,
            to_voxels,
            lambda k: update(k, step, masks, sums),
            to_waves,
            from_plane,
        ]
        for stage in stages:
            for k in range(4):
                stage(k)
        correct(later, active, sums)
        return carry

    for arrival in arrivals[5:]:
        arrival.wait()
    sums = [None] * 6
    for k in range(4):
        update(k, None, (None, None, None), sums)
        to_waves(k)
    for k in range(4):
        from_plane(k)
    correct(None, None, sums)
    lax.fori_loop(0, limit - 1, sweep, 0)
    for k in range(4):
        wave_part(k)
    for k in range(4):
        to_plane(k)
        to_voxels(k)
    for k in range(4):
        for pair in range(2):
            place = slice((k * 2 + pair) * 16, (k * 2 + pair + 1) * 16)
            for c in range(6):
                put = slice((c * 2 + pair) * 16, (c * 2 + pair + 1) * 16)
                state[0, c, place, :] = state[0, c, place, :] + back[k, put, :]

    def gather(x, sums):
        place = pl.ds(pl.multiple_of(x * 2 * SLOTS, 2 * SLOTS), 2 * SLOTS)
        out = []
        for half in range(2):
            strain = [state[1 - half, c, place, :] for c in range(6)]
            shear = start[half, 6, place, :]
            pressure = start[half, 7, place, :] * ((strain[0] + strain[1]) + strain[2])
            for c in range(6):
                stress = shear * strain[c]
                if c < 3:
                    stress = stress + pressure
                stress = stress[:SLOTS] + stress[SLOTS:]
                out.append(sums[6 * half + c] + (stress[:, :LANES] + stress[:, LANES:]))
        return tuple(out)

    sums = lax.fori_loop(
        0, NV // 2, gather, tuple(jnp.zeros((SLOTS, LANES), f32) for _ in range(12))
    )
    for half in range(2):
        for c in range(6):
            mean = jnp.sum(sums[6 * half + c], axis=1, keepdims=True)
            mean = mean * (1.0 / (VOX * MANDEL[c]))
            means[half, c] = jnp.broadcast_to(mean, (SLOTS, LANES))
    for block in range(2):
        for c in range(6):
            base = c * RVES + block * SLOTS
            rows[base : base + SLOTS, :] = pick(means[0, c], means[1, c], places[2 + block])

    stress_rows = jnp.concatenate([rows[0:96, :], jnp.zeros((32, LANES), f32)], axis=0)
    force = exact(line_tables[NV * 12 + 96 :, :], stress_rows)
    lane_of = lax.broadcasted_iota(jnp.int32, (16, LANES), 1)
    right = []
    for low in range(2):
        block = jnp.zeros((16, LANES), f32)
        for i in range(3):
            block = jnp.where(lane_of == 3 * low + i, force[16 * i : 16 * i + 16], block)
        right.append(block)
    block = jnp.zeros((16, LANES), f32)
    for c in range(6):
        block = jnp.where(lane_of == 6 + c, rows[c * RVES : (c + 1) * RVES, :], block)
    right.append(block)
    right.append(jnp.zeros((80, LANES), f32))
    target = [jnp.where((n & 1) == 0, n >> 1, -1) for n in nodes]
    target += [jnp.where((n & 1) == 1, n >> 1, -1) for n in nodes]
    target += [elem[0] * RVES + routing[r] for r in range(RVES)]
    wanted = from_scalars(target, 1, (LANES, LANES))
    taken = (lax.broadcasted_iota(jnp.int32, (LANES, LANES), 0) == wanted).astype(f32)
    sent[...] = exact(taken, jnp.concatenate(right, axis=0)).reshape(LANES, 1, LANES)


def tables():
    plane_table = np.stack([split_table(table) for table in plane_tables()])
    strain_table, force_table = element_tables()
    line_table = np.zeros((NV * 12 + 96 + 48, LANES), np.float32)
    line_table[: NV * 12] = green_tables().reshape(NV * 12, LANES)
    line_table[NV * 12 : NV * 12 + 96, :48] = strain_table
    line_table[NV * 12 + 96 :, :96] = force_table
    return plane_table, line_table


SMEM = pl.BlockSpec(memory_space=pltpu.SMEM)
VMEM = pl.BlockSpec(memory_space=pltpu.VMEM)
HBM = pl.BlockSpec(memory_space=pltpu.HBM)
VMEM_MIB = 40
SOLVE_MIB = 54
PREPARE_MIB = 61
FINISH_MIB = 61
PARAMS = pltpu.CompilerParams(vmem_limit_bytes=VMEM_MIB * 1024 * 1024)


def of(shape, kind=jnp.float32):
    return jax.ShapeDtypeStruct(shape, kind)


def prepare(counts, fluctuation, phases, damage):
    f32 = jnp.float32
    return pl.pallas_call(
        prepare_kernel,
        out_shape=(
            of((2, 8, ROWS, PLANE)),
            of((6, SLOTS, LANES), jnp.int32),
        ),
        in_specs=[HBM] * 4,
        out_specs=(HBM, HBM),
        scratch_shapes=[
            pltpu.VMEM((2, 8, ROWS, PLANE), f32),
            pltpu.VMEM((6, SLOTS, LANES), jnp.int32),
            pltpu.SMEM((RVES,), jnp.int32),
            pltpu.SMEM((RVES,), jnp.int32),
            pltpu.SMEM((RVES,), jnp.int32),
            pltpu.SMEM((RVES,), jnp.int32),
            pltpu.VMEM((6, RVES, VOX), f32),
            pltpu.VMEM((RVES, VOX), jnp.int32),
            pltpu.VMEM((RVES, VOX), f32),
            pltpu.SemaphoreType.DMA((9,)),
            pltpu.SemaphoreType.DMA((5,)),
        ],
        cost_estimate=pl.CostEstimate(
            flops=8_000_000, bytes_accessed=8_000_000, transcendentals=0
        ),
        compiler_params=pltpu.CompilerParams(vmem_limit_bytes=PREPARE_MIB * 1024 * 1024),
        name="prepare_rves",
    )(counts, fluctuation, phases, damage)


def solve(routing, connectivity, elem, motion, prepared):
    f32 = jnp.float32
    plane_table, line_table = tables()
    return pl.pallas_call(
        sweep_kernel,
        out_shape=(of((2, 6, ROWS, PLANE)), of((2, 6, SLOTS, LANES)), of((LANES, 1, LANES))),
        in_specs=[SMEM] + [HBM] * 7,
        out_specs=(VMEM,) * 3,
        scratch_shapes=[
            pltpu.VMEM((LANES, 1, LANES), f32),
            pltpu.SMEM((RVES,), jnp.int32),
            pltpu.SMEM((2, 8), jnp.int32),
            pltpu.VMEM((6, SLOTS, LANES), jnp.int32),
            pltpu.VMEM(line_table.shape, f32),
            pltpu.VMEM((2, 8, ROWS, PLANE), f32),
            pltpu.VMEM(plane_table.shape, jnp.bfloat16),
            pltpu.VMEM((NV * 12, SLOTS, LANES), f32),
            pltpu.VMEM((96, LANES), f32),
            pltpu.VMEM((4, 2, 192, PLANE), jnp.bfloat16),
            pltpu.VMEM((4, 2, 192, PLANE), jnp.bfloat16),
            pltpu.VMEM((4, 192, PLANE), f32),
            pltpu.VMEM((4, 192, PLANE), f32),
            pltpu.VMEM((6, 4, 4, 2, SLOTS, LANES), f32),
            pltpu.VMEM((6, 4, 4, 2, SLOTS, LANES), f32),
            pltpu.VMEM((6, SLOTS, LANES), f32),
            pltpu.VMEM((6, SLOTS, LANES), f32),
            pltpu.VMEM((2, 6, SLOTS, LANES), f32),
            pltpu.SemaphoreType.DMA((8,)),
        ],
        compiler_params=pltpu.CompilerParams(vmem_limit_bytes=SOLVE_MIB * 1024 * 1024),
        name="solve_rves",
    )(
        elem,
        motion,
        routing,
        connectivity,
        prepared[1],
        jnp.asarray(line_table),
        prepared[0],
        jnp.asarray(plane_table),
    )


def finish(state, macro, places):
    return pl.pallas_call(
        finish_kernel,
        out_shape=of((6, RVES, VOX)),
        in_specs=[HBM] * 3,
        out_specs=HBM,
        scratch_shapes=[
            pltpu.VMEM((2, 6, ROWS, PLANE), jnp.float32),
            pltpu.VMEM((2, 6, SLOTS, LANES), jnp.float32),
            pltpu.VMEM((6, SLOTS, LANES), jnp.int32),
            pltpu.VMEM((6, RVES, VOX), jnp.float32),
            pltpu.SemaphoreType.DMA((6,)),
            pltpu.SemaphoreType.DMA((NV,)),
        ],
        cost_estimate=pl.CostEstimate(
            flops=4_000_000, bytes_accessed=4_000_000, transcendentals=0
        ),
        compiler_params=pltpu.CompilerParams(vmem_limit_bytes=FINISH_MIB * 1024 * 1024),
        name="finish_rves",
    )(state, macro, places)


def exchange(rows):
    return lax.all_to_all(rows, ("elem", "rve"), split_axis=0, concat_axis=0, tiled=True)


def shards(
    displacement,
    connectivity,
    fluctuation,
    phases,
    damage,
    iteration_counts,
    routing,
    external_force,
):
    own = jnp.pad(displacement.T.reshape(1, 1, 6), ((0, 0), (0, 0), (0, LANES - 6)))
    own = jnp.broadcast_to(own, (LANES, 1, LANES))
    motion = exchange(own)
    elem = lax.axis_index("elem").astype(jnp.int32).reshape(1)
    prepared = prepare(
        iteration_counts, jnp.transpose(fluctuation, (1, 0, 2)), phases, damage
    )
    state, macro, sent = solve(routing, connectivity.T, elem, motion, prepared)
    received = exchange(sent)
    fluctuation_out = jnp.transpose(finish(state, macro, prepared[1]), (1, 0, 2))
    residual_force, pool_stress = pl.pallas_call(
        collect_kernel,
        out_shape=(of((2, 3)), of((6, RVES))),
        in_specs=[SMEM, VMEM, VMEM],
        out_specs=(HBM, HBM),
        scratch_shapes=[
            pltpu.VMEM((2, 3), jnp.float32),
            pltpu.VMEM((6, RVES), jnp.float32),
            pltpu.SemaphoreType.DMA((2,)),
        ],
        compiler_params=PARAMS,
        name="collect_results",
    )(elem, received, external_force.T)
    return (residual_force.T, fluctuation_out, pool_stress.T)


def solution(mesh):
    both = ("elem", "rve")
    return jax.shard_map(
        shards,
        mesh=mesh,
        in_specs=(
            P(None, both),
            P(None, both),
            P(both, None, None),
            P(both, None),
            P(both, None),
            P(both),
            P(both),
            P(None, both),
        ),
        out_specs=(P(None, both), P(both, None, None), P(both, None)),
        check_vma=False,
    )
```
